32 devices in a mesh: grp: 2 (over x), samp: 16 (over z, y, core).
Axes of the slice: x: 2, y: 2, z: 4, core: 2. Of those that a mesh axis runs over, the one named last changes fastest.
Arguments:
- genotypes: int32 [32768, 2048], P(('grp', 'samp')), parts along dimension 0, may hold values from 0 to 2
- probe_signs: int32 [32, 32768], P(None, ('grp', 'samp')), parts along dimension 1, may hold values from 0 to 1
- phenotype: float32 [32768], P(('grp', 'samp')), parts along dimension 0, may hold values from -6 to 6
- marker_mean: float32 [2048], replicated, may hold values from 0.2 to 1.8
- marker_scale: float32 [2048], replicated, may hold values from 0.5 to 4
- marker_bin: int32 [2048], replicated, may hold values from 0 to 15, as said below
Outputs:
- products: float32 [16, 33, 32768], P(None, None, ('grp', 'samp')), parts along dimension 2
- gram: float32 [32, 16, 33], P('grp'), parts along dimension 0
The draws below stay inside these ranges and needn't reach their ends.
There are 2 independent parts, one for each index of `grp`. The reference program is written for one: setup_inputs(seed, part) draws one part's arguments, and reference() takes and returns one part's arrays. A program takes and returns all parts, laid end to end along the dimension named above; an argument that names none is the same for every part. Nothing has to cross between parts.
Inputs may be any that keep to these rules, and one draw needn't show every extreme that they name: `marker_bin`: every bin holds exactly 128 markers.
All inputs are finite; a program needn't handle non-finite values.
Results may differ from the reference program's by a relative error of at most 0.0001.
Values sent between devices are 32-bit elements; how exact they have to be, the bound alone decides.
No kernel may reach another device: no remote copies, remote signals or barrier semaphores. Data moves between devices by JAX's collectives and lax.ppermute only.
A program may use at most 128 MiB of HBM per device.

```python
import math
import jax
import jax.numpy as jnp
from jax import lax

BINS = 16
M_BIN = 128
PROBES = 32
MARKERS = 2048
VECS = 33
NSAMP = 16384


def draw_marker_bin(key, part):
    return (jax.random.permutation(key, MARKERS) // M_BIN).astype(jnp.int32)


def plant(entries, own_key, least, largest):
    index_at = [jax.random.randint(jax.random.fold_in(own_key, axis), (), 0, length) for axis, length in enumerate(entries.shape)]
    longest = entries.shape.index(max(entries.shape))
    next_to = index_at[:longest] + [(index_at[longest] + 1) % entries.shape[longest]] + index_at[longest + 1:]
    return entries.at[tuple(index_at)].set(least).at[tuple(next_to)].set(largest)


def block_levels(rng, dims, shards, low, top_value):
    def one(dim, blocks):
        steps = jax.random.uniform(jax.random.fold_in(jax.random.fold_in(rng, 6), dim), (blocks,), jnp.float32, low / len(shards), top_value / len(shards))
        return jnp.repeat(jnp.exp(steps), dims[dim] // blocks).reshape((-1,) + (1,) * (len(dims) - dim - 1))

    loudness = one(*shards[0])
    for cut in shards[1:]:
        loudness = loudness * one(*cut)
    return loudness


def scatter_about(key, dims, spread, limit, shards=(), kind=jnp.bfloat16):
    level = block_levels(key, dims, shards, -0.22, 0.18) if shards else 1.0
    entries = jax.random.normal(key, dims, jnp.float32) * spread * level
    return jnp.minimum(jnp.maximum(entries, -limit), limit).astype(kind)


def setup_inputs(seed: int = 0, part: int = 0) -> dict:
    key_of = jax.random.split(jax.random.key(seed), 7)
    part_keys = jax.random.split(jax.random.fold_in(key_of[6], part), 7)
    return {
        "genotypes": plant(jax.random.randint(part_keys[0], (NSAMP, MARKERS), 0, 3), jax.random.fold_in(part_keys[0], 1), 0, 2).astype(jnp.int32),
        "probe_signs": plant(jax.random.randint(part_keys[1], (PROBES, NSAMP), 0, 2), jax.random.fold_in(part_keys[1], 1), 0, 1).astype(jnp.int32),
        "phenotype": scatter_about(part_keys[2], (NSAMP,), 1.0, 6.0, ((0, 16),), jnp.float32),
        "marker_mean": jnp.clip(jax.random.uniform(key_of[3], (MARKERS,), jnp.float32, 0.2, 1.8), 0.2, 1.8),
        "marker_scale": jnp.clip(jnp.exp(jax.random.uniform(key_of[4], (MARKERS,), jnp.float32, math.log(0.5), math.log(4.0))), 0.5, 4.0),
        "marker_bin": draw_marker_bin(jax.random.fold_in(key_of[6], 71), part),
    }


def reference(genotypes, probe_signs, phenotype, marker_mean, marker_scale, marker_bin):
    order = jnp.argsort(marker_bin, stable=True).astype(jnp.int32)
    picked = jnp.take(genotypes, order, axis=1).astype(jnp.float32)
    standard = (picked - marker_mean[order]) * marker_scale[order]
    vectors = jnp.concatenate([(2 * probe_signs - 1).astype(jnp.float32), phenotype[None, :].astype(jnp.float32)], axis=0)
    scores = jnp.dot(standard.T, vectors.T, precision=lax.Precision.HIGHEST, preferred_element_type=jnp.float32)
    scores = scores / jnp.sqrt(jnp.float32(NSAMP))
    blocks = standard.reshape(NSAMP, BINS, M_BIN)
    weights = scores.reshape(BINS, M_BIN, VECS)
    products = jnp.einsum('skm,kmr->krs', blocks, weights, precision=lax.Precision.HIGHEST) / jnp.sqrt(jnp.float32(M_BIN))
    gram = jnp.einsum('krs,lrs->klr', products, products, precision=lax.Precision.HIGHEST) / jnp.float32(NSAMP)
    return (products, gram)
```

```python
import functools

import jax
import jax.numpy as jnp
from jax import lax
from jax.experimental import pallas as pl
from jax.experimental.pallas import tpu as pltpu
from jax.sharding import PartitionSpec as P

BINS = 16
LANES = 128
F32 = jnp.float32
BF16 = jnp.bfloat16


def two_parts(x):
    hi = x.astype(BF16)
    return hi, (x - hi.astype(F32)).astype(BF16)


def scores_kernel(core_ref, geno_ref, signs_ref, pheno_ref, mean_ref, scale_ref, own_ref, other_ref, acc, sums, *, steps, norm):
    step = pl.program_id(0)
    probes = signs_ref.shape[0]
    markers = geno_ref.shape[1]
    half = probes // 2

    @pl.when(step == 0)
    def _():
        acc[...] = jnp.zeros_like(acc)
        sums[...] = jnp.zeros_like(sums)

    signs = (2 * signs_ref[...] - 1).astype(F32)
    pheno = pheno_ref[...]
    high = pheno.astype(BF16).astype(F32)
    rest = pheno - high
    middle = rest.astype(BF16).astype(F32)
    low = rest - middle
    tail = jnp.zeros((5, pheno.shape[1]), F32)
    vectors = jnp.concatenate([signs, high, middle, low, tail], axis=0)
    acc[...] += jnp.dot(vectors.astype(BF16), geno_ref[...].astype(F32).astype(BF16), preferred_element_type=F32)
    sums[...] += jnp.sum(vectors, axis=1, keepdims=True)

    @pl.when(step == steps - 1)
    def _():
        scale = scale_ref[...] * norm
        acc[...] = (acc[...] - mean_ref[...] * sums[:, :1]) * scale
        core = core_ref[0]
        row = acc[probes : probes + 1, :] + acc[probes + 1 : probes + 2, :] + acc[probes + 2 : probes + 3, :]
        tiles = markers // LANES // 2
        for ref, side in ((own_ref, core), (other_ref, 1 - core)):
            ref[:, :markers] = acc[pl.ds(pl.multiple_of(side * half, half), half), :]
            ref[:, markers:] = jnp.zeros((half, LANES), F32)
            for t in range(tiles):
                low_part = row[:, t * LANES : (t + 1) * LANES]
                high_part = row[:, (tiles + t) * LANES : (tiles + t + 1) * LANES]
                ref[t : t + 1, markers:] = jnp.where(side == 0, low_part, high_part)


def products_kernel(core_ref, own_ref, other_ref, geno_ref, mean_ref, scale_ref, bin_ref, out_ref, gram_ref, w_hi, w_lo, shift, acc, *, steps, norm, gram_norm):
    step = pl.program_id(0)
    half = own_ref.shape[0]
    probes = 2 * half
    markers = geno_ref.shape[1]
    groups = probes // 8

    @pl.when(step == 0)
    def _():
        core = core_ref[0]
        acc[...] = jnp.zeros_like(acc)
        scale = scale_ref[...] * norm
        mean = mean_ref[...]
        inside = bin_ref[...] == lax.broadcasted_iota(jnp.int32, (BINS, markers), 0)
        member = inside.astype(F32)

        def place(row, at):
            weighted = member * row
            shift[pl.ds(at, BINS), :] = jnp.broadcast_to(jnp.sum(weighted * mean, axis=1, keepdims=True), (BINS, LANES))
            hi, lo = two_parts(weighted)
            w_hi[pl.ds(at, BINS), :] = hi
            w_lo[pl.ds(at, BINS), :] = lo

        for ref, side in ((own_ref, core), (other_ref, 1 - core)):
            rows = ref[:, :markers] * scale
            for r in range(half):
                place(rows[r : r + 1, :], pl.multiple_of((side * half + r) * BINS, BINS))
        tiles = markers // LANES // 2
        mine = [own_ref[t : t + 1, markers:] for t in range(tiles)]
        theirs = [other_ref[t : t + 1, markers:] for t in range(tiles)]
        first = [jnp.where(core == 0, a, b) for a, b in zip(mine, theirs)]
        second = [jnp.where(core == 0, b, a) for a, b in zip(mine, theirs)]
        place(jnp.concatenate(first + second, axis=1) * scale, probes * BINS)

    geno = geno_ref[...].astype(F32).astype(BF16)
    nt = (((1,), (1,)), ((), ()))
    dot = functools.partial(lax.dot_general, dimension_numbers=nt, preferred_element_type=F32)
    products = dot(w_hi[...], geno) + dot(w_lo[...], geno) - shift[:, :1]
    out_ref[...] = products.reshape(out_ref.shape)
    hi, lo = two_parts(products)
    for g in range(groups):
        a, b = hi[g * LANES : (g + 1) * LANES], lo[g * LANES : (g + 1) * LANES]
        acc[g * LANES : (g + 1) * LANES, :] += dot(a, a) + dot(a, b) + dot(b, a)
    a, b = hi[groups * LANES :], lo[groups * LANES :]
    acc[groups * LANES :, :BINS] += dot(a, a) + dot(a, b) + dot(b, a)

    @pl.when(step == steps - 1)
    def _():
        column = lax.broadcasted_iota(jnp.int32, (BINS, LANES), 1)
        for g in range(groups):
            total = jnp.zeros((BINS, LANES), F32)
            for r in range(8):
                block = acc[g * LANES + r * BINS : g * LANES + (r + 1) * BINS, :]
                total = jnp.where(column // BINS == r, block, total)
            gram_ref[:, g * LANES : (g + 1) * LANES] = total * gram_norm
        gram_ref[:, groups * LANES :] = acc[groups * LANES :, :] * gram_norm


def exchange(x, pairs):
    return lax.ppermute(x, "samp", pairs)


def shards(genotypes, probe_signs, phenotype, marker_mean, marker_scale, marker_bin):
    samples, markers = genotypes.shape
    probes = probe_signs.shape[0]
    half = probes // 2
    devices = lax.axis_size("samp")
    total = samples * devices
    core = lax.rem(lax.axis_index("samp"), 2).reshape(1)
    mean = marker_mean.reshape(1, markers)
    scale = marker_scale.reshape(1, markers)
    bins = marker_bin.reshape(1, markers)

    block = min(samples, 256)
    steps = samples // block
    whole = lambda i: (0, 0)
    row = pl.BlockSpec((1, markers), whole)
    smem = pl.BlockSpec(memory_space=pltpu.SMEM)
    part = jax.ShapeDtypeStruct((half, markers + LANES), F32)
    own, other = pl.pallas_call(
        functools.partial(scores_kernel, steps=steps, norm=total ** -0.5),
        grid=(steps,),
        out_shape=(part, part),
        in_specs=[
            smem,
            pl.BlockSpec((block, markers), lambda i: (i, 0)),
            pl.BlockSpec((probes, block), lambda i: (0, i)),
            pl.BlockSpec((1, block), lambda i: (0, i)),
            row,
            row,
        ],
        out_specs=(pl.BlockSpec(part.shape, whole), pl.BlockSpec(part.shape, whole)),
        scratch_shapes=[pltpu.VMEM((probes + 8, markers), F32), pltpu.VMEM((probes + 8, LANES), F32)],
        compiler_params=pltpu.CompilerParams(vmem_limit_bytes=48 * 2**20),
        name="scores",
    )(core, genotypes, probe_signs, phenotype.reshape(1, samples), mean, scale)

    flips = [1 << b for b in range(1, devices.bit_length() - 1)]
    cores = [(i, i ^ 1) for i in range(devices)]
    own = own + exchange(other, cores)
    for s in range(len(flips)):
        even, odd = flips[s], flips[s - 1]
        own = own + exchange(own, [(i, i ^ (odd if i % 2 else even)) for i in range(devices)])
    other = exchange(own, cores)

    rows = (probes + 1) * BINS
    gram_wide = (probes // 8 + 1) * LANES
    products, gram = pl.pallas_call(
        functools.partial(products_kernel, steps=steps, norm=(markers // BINS) ** -0.5, gram_norm=1.0 / total),
        grid=(steps,),
        out_shape=(
            jax.ShapeDtypeStruct((probes + 1, BINS, samples), F32),
            jax.ShapeDtypeStruct((BINS, gram_wide), F32),
        ),
        in_specs=[
            smem,
            pl.BlockSpec(part.shape, whole),
            pl.BlockSpec(part.shape, whole),
            pl.BlockSpec((block, markers), lambda i: (i, 0)),
            row,
            row,
            row,
        ],
        out_specs=(
            pl.BlockSpec((probes + 1, BINS, block), lambda i: (0, 0, i)),
            pl.BlockSpec((BINS, gram_wide), whole),
        ),
        scratch_shapes=[
            pltpu.VMEM((rows, markers), BF16),
            pltpu.VMEM((rows, markers), BF16),
            pltpu.VMEM((rows, LANES), F32),
            pltpu.VMEM((rows, LANES), F32),
        ],
        compiler_params=pltpu.CompilerParams(vmem_limit_bytes=48 * 2**20),
        name="products",
    )(core, own, other, genotypes, mean, scale, bins)

    for flip in [1] + flips:
        gram = gram + exchange(gram, [(i, i ^ flip) for i in range(devices)])
    gram = gram[:, : (probes + 1) * BINS].reshape(BINS, probes + 1, BINS)
    return (products.transpose(1, 0, 2), gram.transpose(0, 2, 1))


def solution(mesh):
    in_specs = (
        P(("grp", "samp"), None),
        P(None, ("grp", "samp")),
        P(("grp", "samp")),
        P(),
        P(),
        P(),
    )
    out_specs = (P(None, None, ("grp", "samp")), P("grp", None, None))
    return jax.shard_map(shards, mesh=mesh, in_specs=in_specs, out_specs=out_specs, check_vma=False)
```

```python
import functools

import jax
import jax.numpy as jnp
from jax import lax
from jax.experimental import pallas as pl
from jax.experimental.pallas import tpu as pltpu
from jax.sharding import PartitionSpec as P

BINS = 16
LANES = 128
GROUP = LANES // BINS
F32 = jnp.float32
BF16 = jnp.bfloat16
MIB = 2**20

dot_nt = functools.partial(lax.dot_general, dimension_numbers=(((1,), (1,)), ((), ())), preferred_element_type=F32)


def two_parts(x):
    hi = x.astype(BF16)
    return hi, (x - hi.astype(F32)).astype(BF16)


def scores_kernel(core_ref, geno_hbm, signs_hbm, pheno_hbm, mean_hbm, scale_hbm, own_ref, other_ref, raw, signs, pheno, mean, scale, acc, raw_sems, sems, *, chunk, norm):
    samples, markers = raw.shape
    probes = signs.shape[0]
    half = probes // 2
    chunks = samples // chunk
    pairs = ((signs_hbm, signs), (pheno_hbm, pheno), (mean_hbm, mean), (scale_hbm, scale))
    small = [pltpu.make_async_copy(src, dst, sems.at[i]) for i, (src, dst) in enumerate(pairs)]
    rows = [slice(c * chunk, (c + 1) * chunk) for c in range(chunks)]
    large = [pltpu.make_async_copy(geno_hbm.at[s], raw.at[s], raw_sems.at[c]) for c, s in enumerate(rows)]
    for copy in small[:2] + large + small[2:]:
        copy.start()
    small[0].wait()
    small[1].wait()
    high = pheno[...].astype(BF16).astype(F32)
    rest = pheno[...] - high
    middle = rest.astype(BF16).astype(F32)
    tail = jnp.zeros((5, samples), F32)
    vectors = jnp.concatenate([(2 * signs[...] - 1).astype(F32), high, middle, rest - middle, tail], axis=0)
    sums = jnp.sum(vectors, axis=1, keepdims=True)
    vectors = vectors.astype(BF16)
    for c, s in enumerate(rows):
        large[c].wait()
        part = jnp.dot(vectors[:, s], raw[s].astype(F32).astype(BF16), preferred_element_type=F32)
        if c == 0:
            acc[...] = part
        else:
            acc[...] += part
    small[2].wait()
    small[3].wait()
    acc[...] = (acc[...] - mean[...] * sums) * (scale[...] * norm)
    core = core_ref[0]
    row = acc[probes : probes + 1, :] + acc[probes + 1 : probes + 2, :] + acc[probes + 2 : probes + 3, :]
    tiles = markers // LANES // 2
    for ref, side in ((own_ref, core), (other_ref, 1 - core)):
        ref[:, :markers] = acc[pl.ds(pl.multiple_of(side * half, half), half), :]
        ref[:, markers:] = jnp.zeros((half, LANES), F32)
        for t in range(tiles):
            low_part = row[:, t * LANES : (t + 1) * LANES]
            high_part = row[:, (tiles + t) * LANES : (tiles + t + 1) * LANES]
            ref[half - tiles + t : half - tiles + t + 1, markers:] = jnp.where(side == 0, low_part, high_part)


def narrow_kernel(geno_ref, out_ref):
    out_ref[...] = geno_ref[...].astype(F32).astype(BF16)


def products_kernel(core_ref, own_ref, other_ref, geno_ref, mean_ref, scale_ref, bin_ref, out_ref, gram_ref, weights, prod, sems, *, norm, gram_norm):
    half = own_ref.shape[0]
    probes = 2 * half
    markers = geno_ref.shape[1]
    core = core_ref[0]
    scale = scale_ref[...] * norm
    mean = mean_ref[...]
    member = (bin_ref[...] == lax.broadcasted_iota(jnp.int32, (BINS, markers), 0)).astype(F32)
    tiles = markers // LANES // 2
    mine = [own_ref[half - tiles + t : half - tiles + t + 1, markers:] for t in range(tiles)]
    theirs = [other_ref[half - tiles + t : half - tiles + t + 1, markers:] for t in range(tiles)]
    first = [jnp.where(core == 0, a, b) for a, b in zip(mine, theirs)]
    second = [jnp.where(core == 0, b, a) for a, b in zip(mine, theirs)]
    pheno = jnp.concatenate(first + second, axis=1)

    copies = []
    passes = half // GROUP
    at = 0
    for p in range(passes):
        rows = [ref[p * GROUP + r : p * GROUP + r + 1, :markers] for ref in (own_ref, other_ref) for r in range(GROUP)]
        if p == passes - 1:
            rows.append(pheno)
        count = len(rows) * BINS
        shifts = []
        for r, row in enumerate(rows):
            weighted = member * (row * scale)
            shifts.append(jnp.sum(weighted * mean, axis=1, keepdims=True))
            hi, lo = two_parts(weighted)
            weights[p, r * BINS : (r + 1) * BINS, :] = hi
            weights[p, count + r * BINS : count + (r + 1) * BINS, :] = lo
        both = dot_nt(weights[p, : 2 * count, :], geno_ref[...])
        products = both[:count] + both[count:] - jnp.concatenate(shifts, axis=0)
        prod[at : at + len(rows)] = products.reshape(len(rows), BINS, products.shape[1])
        starts = [pl.multiple_of(side * half + p * GROUP, GROUP) for side in (core, 1 - core)]
        spans = [(at + i * GROUP, GROUP, start) for i, start in enumerate(starts)]
        if p == passes - 1:
            spans.append((at + 2 * GROUP, 1, probes))
        for source, size, start in spans:
            copy = pltpu.make_async_copy(prod.at[pl.ds(source, size)], out_ref.at[pl.ds(start, size)], sems.at[len(copies)])
            copy.start()
            copies.append(copy)
        column = lax.broadcasted_iota(jnp.int32, (BINS, LANES), 1) // BINS
        for i, start in enumerate(starts):
            a, b = two_parts(products[i * LANES : (i + 1) * LANES])
            square = dot_nt(a, a) + dot_nt(a, b) + dot_nt(b, a)
            total = square[:BINS]
            for r in range(1, GROUP):
                total = jnp.where(column == r, square[r * BINS : (r + 1) * BINS], total)
            gram_ref[:, pl.ds(pl.multiple_of(start * BINS, LANES), LANES)] = total * gram_norm
        if p == passes - 1:
            a, b = two_parts(products[2 * LANES :])
            square = dot_nt(a, a) + dot_nt(a, b) + dot_nt(b, a)
            gram_ref[:, probes * BINS : (probes + 1) * BINS] = square * gram_norm
            gram_ref[:, (probes + 1) * BINS :] = jnp.zeros((BINS, LANES - BINS), F32)
        at += len(rows)
    for copy in copies:
        copy.wait()


def parity(i):
    return bin(i).count("1") % 2


def exchange(x, flip):
    return lax.ppermute(x, "samp", [(i, i ^ flip) for i in range(lax.axis_size("samp"))])


def shards(genotypes, probe_signs, phenotype, marker_mean, marker_scale, marker_bin):
    samples, markers = genotypes.shape
    probes = probe_signs.shape[0]
    half = probes // 2
    devices = lax.axis_size("samp")
    total = samples * devices
    core = (lax.population_count(lax.axis_index("samp")) & 1).astype(jnp.int32).reshape(1)
    mean = marker_mean.reshape(1, markers)
    scale = marker_scale.reshape(1, markers)
    bins = marker_bin.reshape(1, markers)
    smem = pl.BlockSpec(memory_space=pltpu.SMEM)
    vmem = pl.BlockSpec(memory_space=pltpu.VMEM)
    hbm = pl.BlockSpec(memory_space=pl.ANY)

    chunk = min(samples, 256)
    part = jax.ShapeDtypeStruct((half, markers + LANES), F32)
    own, other = pl.pallas_call(
        functools.partial(scores_kernel, chunk=chunk, norm=total**-0.5),
        out_shape=(part, part),
        in_specs=[smem, hbm, hbm, hbm, hbm, hbm],
        out_specs=(vmem, vmem),
        scratch_shapes=[
            pltpu.VMEM((samples, markers), jnp.int32),
            pltpu.VMEM((probes, samples), jnp.int32),
            pltpu.VMEM((1, samples), F32),
            pltpu.VMEM((1, markers), F32),
            pltpu.VMEM((1, markers), F32),
            pltpu.VMEM((probes + 8, markers), F32),
            pltpu.SemaphoreType.DMA((samples // chunk,)),
            pltpu.SemaphoreType.DMA((4,)),
        ],
        compiler_params=pltpu.CompilerParams(vmem_limit_bytes=62 * MIB),
        name="scores",
    )(core, genotypes, probe_signs, phenotype.reshape(1, samples), mean, scale)

    narrow = pl.pallas_call(
        narrow_kernel,
        out_shape=jax.ShapeDtypeStruct((samples, markers), BF16),
        in_specs=[vmem],
        out_specs=vmem,
        cost_estimate=pl.CostEstimate(flops=0, bytes_accessed=samples * markers * 6, transcendentals=0),
        compiler_params=pltpu.CompilerParams(vmem_limit_bytes=16 * MIB),
        name="narrow",
    )(genotypes)

    flips = [1 << b for b in range(1, devices.bit_length() - 1)]
    own = own + exchange(other, 1)
    for s in range(len(flips)):
        if s == len(flips) - 1:
            own, narrow = lax.optimization_barrier((own, narrow))
        even, odd = flips[s] | 1, flips[(s + 1) % len(flips)] | 1
        own = own + lax.ppermute(own, "samp", [(i, i ^ (odd if parity(i) else even)) for i in range(devices)])
    other = exchange(own, 1)

    gram_wide = (probes // GROUP + 1) * LANES
    passes = half // GROUP
    products, gram = pl.pallas_call(
        functools.partial(products_kernel, norm=(markers // BINS) ** -0.5, gram_norm=1.0 / total),
        out_shape=(
            jax.ShapeDtypeStruct((probes + 1, BINS, samples), F32),
            jax.ShapeDtypeStruct((BINS, gram_wide), F32),
        ),
        in_specs=[smem, vmem, vmem, vmem, vmem, vmem, vmem],
        out_specs=(hbm, vmem),
        scratch_shapes=[
            pltpu.VMEM((passes, 2 * (2 * GROUP + 1) * BINS, markers), BF16),
            pltpu.VMEM((probes + 1, BINS, samples), F32),
            pltpu.SemaphoreType.DMA((2 * passes + 1,)),
        ],
        compiler_params=pltpu.CompilerParams(vmem_limit_bytes=36 * MIB),
        name="products",
    )(core, own, other, narrow, mean, scale, bins)

    gram = gram + exchange(gram, 1)
    rest = flips
    while rest:
        if len(rest) > 1:
            near, far, both = (exchange(gram, f | 1) for f in (rest[0], rest[1], rest[0] | rest[1]))
            gram = (gram + near) + (far + both)
        else:
            gram = gram + exchange(gram, rest[0] | 1)
        rest = rest[2:]
    gram = gram[:, : (probes + 1) * BINS].reshape(BINS, probes + 1, BINS)
    return (products.transpose(1, 0, 2), gram.transpose(0, 2, 1))


def solution(mesh):
    in_specs = (
        P(("grp", "samp"), None),
        P(None, ("grp", "samp")),
        P(("grp", "samp")),
        P(),
        P(),
        P(),
    )
    out_specs = (P(None, None, ("grp", "samp")), P("grp", None, None))
    return jax.shard_map(shards, mesh=mesh, in_specs=in_specs, out_specs=out_specs, check_vma=False)
```

```python
import functools

import jax
import jax.numpy as jnp
from jax import lax
from jax.experimental import pallas as pl
from jax.experimental.pallas import tpu as pltpu
from jax.sharding import PartitionSpec as P

BINS = 16
LANES = 128
GROUP = LANES // BINS
F32 = jnp.float32
BF16 = jnp.bfloat16
MIB = 2**20

dot_nt = functools.partial(lax.dot_general, dimension_numbers=(((1,), (1,)), ((), ())), preferred_element_type=F32)


def two_parts(x):
    hi = x.astype(BF16)
    return hi, (x - hi.astype(F32)).astype(BF16)


def sign_rows(signs_ref):
    return (2 * signs_ref[...] - 1).astype(F32).astype(BF16)


def pheno_rows(pheno_ref):
    pheno = pheno_ref[...]
    high = pheno.astype(BF16).astype(F32)
    rest = pheno - high
    middle = rest.astype(BF16).astype(F32)
    tail = jnp.zeros((13, pheno.shape[1]), F32)
    return jnp.concatenate([high, middle, rest - middle, tail], axis=0).astype(BF16)


def add_three(x):
    return x[:1] + x[1:2] + x[2:3]


def accumulate(vectors, geno_hbm, narrow_ref, raw, acc, sems, start, chunk):
    samples, markers = raw.shape
    rows = [slice(c * chunk, (c + 1) * chunk) for c in range(samples // chunk)]
    copies = [pltpu.make_async_copy(geno_hbm.at[s, start : start + markers], raw.at[s], sems.at[c]) for c, s in enumerate(rows)]
    for copy in copies:
        copy.start()
    yield
    for c, s in enumerate(rows):
        copies[c].wait()
        narrow = raw[s].astype(F32).astype(BF16)
        narrow_ref[s] = narrow
        part = jnp.dot(vectors()[:, s], narrow, preferred_element_type=F32)
        if c == 0:
            acc[...] = part
        else:
            acc[...] += part
    yield


def place_rows(side, acc, sums, own_ref, other_ref, at):
    half, _ = own_ref.shape
    markers = acc.shape[1]
    for ref, which in ((own_ref, side), (other_ref, 1 - side)):
        ref[:, :markers] = acc[pl.ds(pl.multiple_of(which * half, half), half), :]
        ref[:, at:] = jnp.zeros((half, LANES), F32)
        ref[:1, at : at + half] = jnp.where(which == 0, sums[:, :half], sums[:, half : 2 * half])


def first_sums_kernel(side_ref, geno_hbm, signs_ref, own_ref, other_ref, narrow_ref, raw, acc, sems, *, start, chunk):
    vectors = None
    steps = accumulate(lambda: vectors, geno_hbm, narrow_ref, raw, acc, sems, start, chunk)
    next(steps)
    vectors = sign_rows(signs_ref)
    sums = dot_nt(jnp.ones((8, vectors.shape[1]), BF16), vectors)[:1]
    next(steps)
    place_rows(side_ref[0], acc, sums, own_ref, other_ref, raw.shape[1])


def second_sums_kernel(side_ref, geno_hbm, signs_ref, pheno_ref, first_ref, own_ref, other_ref, narrow_ref, raw, acc, sems, *, start, chunk):
    markers = raw.shape[1]
    probes = signs_ref.shape[0]
    vectors = None
    steps = accumulate(lambda: vectors, geno_hbm, narrow_ref, raw, acc, sems, start, chunk)
    next(steps)
    pheno = pheno_rows(pheno_ref)
    vectors = jnp.concatenate([sign_rows(signs_ref), pheno], axis=0)
    sums = dot_nt(jnp.ones((8, vectors.shape[1]), BF16), vectors)[:1]
    first = add_three(jnp.dot(pheno, first_ref[...], preferred_element_type=F32)[:8])
    next(steps)
    place_rows(side_ref[0], acc, sums, own_ref, other_ref, markers + LANES)
    half = own_ref.shape[0]
    last = sums[:, probes : probes + 1] + sums[:, probes + 1 : probes + 2] + sums[:, probes + 2 : probes + 3]
    row = jnp.concatenate([first, add_three(acc[probes : probes + 8, :])], axis=1)
    for ref in (own_ref, other_ref):
        ref[:1, markers + LANES + half : markers + LANES + half + 1] = last
        for t in range(row.shape[1] // LANES):
            ref[t : t + 1, markers : markers + LANES] = row[:, t * LANES : (t + 1) * LANES]


class Half:
    def __init__(self, mean_ref, scale_ref, bin_ref, geno_ref, start, norm):
        markers = geno_ref.shape[1]
        self.geno = geno_ref
        self.mean = mean_ref[:, start : start + markers]
        scale = scale_ref[:, start : start + markers]
        self.scale = scale * scale * norm
        self.member = (bin_ref[:, start : start + markers] == lax.broadcasted_iota(jnp.int32, (BINS, markers), 0)).astype(F32)

    def scores(self, sums, total):
        return (sums - self.mean * total) * self.scale

    def probe_scores(self, ref):
        markers = self.mean.shape[1]
        at = ref.shape[1] - LANES
        return [self.scores(ref[r : r + 1, :markers], ref[:1, at + r : at + r + 1]) for r in range(ref.shape[0])]

    def products(self, rows, weights):
        shifts = []
        count = len(rows) * BINS
        for r, row in enumerate(rows):
            weighted = self.member * row
            shifts.append(jnp.sum(weighted * self.mean, axis=1, keepdims=True))
            hi, lo = two_parts(weighted)
            weights[r * BINS : (r + 1) * BINS, :] = hi
            weights[count + r * BINS : count + (r + 1) * BINS, :] = lo
        both = dot_nt(weights[: 2 * count, :], self.geno[...])
        return both[:count] + both[count:] - jnp.concatenate(shifts, axis=0)


def square_of(products):
    count = products.shape[0]
    hi, lo = two_parts(products)
    both = dot_nt(jnp.concatenate([hi, lo], axis=0), hi)
    return both[:count] + (both[count:] + both[count:].T)


def gram_of(products, gram_norm):
    parts = []
    column = lax.broadcasted_iota(jnp.int32, (BINS, LANES), 1) // BINS
    for g in range(products.shape[0] // LANES):
        square = square_of(products[g * LANES : (g + 1) * LANES])
        total = square[:BINS]
        for r in range(1, GROUP):
            total = jnp.where(column == r, square[r * BINS : (r + 1) * BINS], total)
        parts.append(total * gram_norm)
    return jnp.concatenate(parts, axis=1)


def part_kernel(own_a, geno_a, mean_ref, scale_ref, bin_ref, part_ref, weights, *, norm):
    first = Half(mean_ref, scale_ref, bin_ref, geno_a, 0, norm)
    part_ref[...] = first.products(first.probe_scores(own_a), weights)


def own_kernel(side_ref, part_ref, other_a, own_b, geno_a, geno_b, mean_ref, scale_ref, bin_ref, out_ref, gram_ref, other_ref, weights, prod, sems, *, norm, gram_norm):
    half = own_b.shape[0]
    count = half * BINS
    markers = geno_a.shape[1]
    samples = geno_a.shape[0]
    first = Half(mean_ref, scale_ref, bin_ref, geno_a, 0, norm)
    second = Half(mean_ref, scale_ref, bin_ref, geno_b, markers, norm)
    tiles = markers // LANES
    pheno = [own_b[t : t + 1, markers : markers + LANES] for t in range(2 * tiles)]
    total = own_b[:1, markers + LANES + half : markers + LANES + half + 1]
    rows_b = second.probe_scores(own_b) + [second.scores(jnp.concatenate(pheno[tiles:], axis=1), total)]
    rows_a = first.probe_scores(other_a) + [first.scores(jnp.concatenate(pheno[:tiles], axis=1), total)]
    parts_b = second.products(rows_b, weights.at[0])
    mine = part_ref[...] + parts_b[:count]
    prod[:half] = mine.reshape(half, BINS, samples)
    copies = [pltpu.make_async_copy(prod.at[pl.ds(0, half)], out_ref.at[pl.ds(pl.multiple_of(side_ref[0] * half, half), half)], sems.at[0])]
    copies[0].start()
    gram_ref[:, : half * BINS] = gram_of(mine, gram_norm)
    parts_a = first.products(rows_a, weights.at[1])
    other_ref[...] = parts_a[:count]
    last = parts_a[count:] + parts_b[count:]
    prod[half : half + 1] = last.reshape(1, BINS, samples)
    copies.append(pltpu.make_async_copy(prod.at[pl.ds(half, 1)], out_ref.at[pl.ds(2 * half, 1)], sems.at[1]))
    copies[1].start()
    gram_ref[:, half * BINS : (half + 1) * BINS] = square_of(last) * gram_norm
    gram_ref[:, (half + 1) * BINS :] = jnp.zeros((BINS, LANES - BINS), F32)
    for copy in copies:
        copy.wait()


def other_kernel(side_ref, part_ref, other_b, geno_b, mean_ref, scale_ref, bin_ref, own_gram_ref, _, out_ref, gram_ref, weights, prod, sems, *, norm, gram_norm):
    half = other_b.shape[0]
    wide = half * BINS
    samples, markers = geno_b.shape
    side = side_ref[0]
    second = Half(mean_ref, scale_ref, bin_ref, geno_b, markers, norm)
    rows = second.probe_scores(other_b)
    products = part_ref[...] + second.products(rows, weights)
    prod[...] = products.reshape(half, BINS, samples)
    copy = pltpu.make_async_copy(prod, out_ref.at[pl.ds(pl.multiple_of((1 - side) * half, half), half)], sems.at[0])
    copy.start()
    gram_ref[:, pl.ds(pl.multiple_of((1 - side) * wide, wide), wide)] = gram_of(products, gram_norm)
    gram_ref[:, pl.ds(pl.multiple_of(side * wide, wide), wide)] = own_gram_ref[:, :wide]
    gram_ref[:, 2 * wide :] = own_gram_ref[:, wide:]
    copy.wait()


def parity(i):
    return bin(i).count("1") % 2


def exchange(x, even, odd=None):
    pairs = [(i, i ^ (even if odd is None or not parity(i) else odd)) for i in range(lax.axis_size("samp"))]
    return lax.ppermute(x, "samp", pairs)


def shards(genotypes, probe_signs, phenotype, marker_mean, marker_scale, marker_bin):
    samples, markers = genotypes.shape
    probes = probe_signs.shape[0]
    half = probes // 2
    devices = lax.axis_size("samp")
    total = samples * devices
    side = (lax.population_count(lax.axis_index("samp")) & 1).astype(jnp.int32).reshape(1)
    markers_info = [x.reshape(1, markers) for x in (marker_mean, marker_scale, marker_bin)]
    pheno = phenotype.reshape(1, samples)
    smem = pl.BlockSpec(memory_space=pltpu.SMEM)
    vmem = pl.BlockSpec(memory_space=pltpu.VMEM)
    hbm = pl.BlockSpec(memory_space=pl.ANY)

    width = markers // 2
    chunk = min(samples, 256)
    narrow = jax.ShapeDtypeStruct((samples, width), BF16)

    def sums(kernel, start, name, extra, rows, *operands):
        part = jax.ShapeDtypeStruct((half, width + extra), F32)
        return pl.pallas_call(
            functools.partial(kernel, start=start, chunk=chunk),
            out_shape=(part, part, narrow),
            in_specs=[smem, hbm] + [vmem] * (len(operands) - 2),
            out_specs=(vmem, vmem, vmem),
            scratch_shapes=[
                pltpu.VMEM((samples, width), jnp.int32),
                pltpu.VMEM((rows, width), F32),
                pltpu.SemaphoreType.DMA((samples // chunk,)),
            ],
            cost_estimate=pl.CostEstimate(flops=2 * rows * samples * width, bytes_accessed=6 * samples * width, transcendentals=0),
            compiler_params=pltpu.CompilerParams(vmem_limit_bytes=47 * MIB),
            name=name,
        )(*operands)

    flips = [1 << b for b in range(1, devices.bit_length() - 1)]
    own_a, other_a, narrow_a = sums(first_sums_kernel, 0, "sums_first", LANES, probes, side, genotypes, probe_signs)
    own_b, other_b, narrow_b = sums(
        second_sums_kernel, width, "sums_second", 2 * LANES, probes + 16, side, genotypes, probe_signs, pheno, narrow_a
    )
    own_a = own_a + exchange(other_a, 1)
    own_b = own_b + exchange(other_b, 1)
    received = None
    for s in range(len(flips)):
        even, odd = flips[s] | 1, flips[(s + 1) % len(flips)] | 1
        own_a = own_a + exchange(own_a, even, odd)
        if received is not None:
            own_b = own_b + received
        received = exchange(own_b, even, odd)

    norm = (total * (markers // BINS)) ** -0.5
    gram_norm = 1.0 / total
    rows = half * BINS

    def work(count):
        return pl.CostEstimate(flops=4 * count * samples * width, bytes_accessed=4 * rows * samples, transcendentals=0)

    params = pltpu.CompilerParams(vmem_limit_bytes=32 * MIB)
    part = jax.ShapeDtypeStruct((rows, samples), F32)
    weights = pltpu.VMEM((2 * rows, width), BF16)
    products = jax.ShapeDtypeStruct((probes + 1, BINS, samples), F32)

    other_a = exchange(own_a, 1)
    own_part = pl.pallas_call(
        functools.partial(part_kernel, norm=norm),
        out_shape=part,
        in_specs=[vmem] * 5,
        out_specs=vmem,
        scratch_shapes=[weights],
        cost_estimate=work(rows),
        compiler_params=params,
        name="products_part",
    )(own_a, narrow_a, *markers_info)
    own_b, received, own_part = lax.optimization_barrier((own_b, received, own_part))
    own_b = own_b + received
    other_b = exchange(own_b, 1)
    products, gram, other_part = pl.pallas_call(
        functools.partial(own_kernel, norm=norm, gram_norm=gram_norm),
        out_shape=(products, jax.ShapeDtypeStruct((BINS, rows + LANES), F32), part),
        in_specs=[smem] + [vmem] * 8,
        out_specs=(hbm, vmem, vmem),
        scratch_shapes=[
            pltpu.VMEM((2, 2 * (rows + BINS), width), BF16),
            pltpu.VMEM((half + 1, BINS, samples), F32),
            pltpu.SemaphoreType.DMA((2,)),
        ],
        cost_estimate=work(2 * rows),
        compiler_params=params,
        name="products_own",
    )(side, own_part, other_a, own_b, narrow_a, narrow_b, *markers_info)
    products, gram = pl.pallas_call(
        functools.partial(other_kernel, norm=norm, gram_norm=gram_norm),
        out_shape=(products, jax.ShapeDtypeStruct((BINS, 2 * rows + LANES), F32)),
        in_specs=[smem] + [vmem] * 7 + [hbm],
        out_specs=(hbm, vmem),
        scratch_shapes=[weights, pltpu.VMEM((half, BINS, samples), F32), pltpu.SemaphoreType.DMA((1,))],
        input_output_aliases={8: 0},
        cost_estimate=work(rows),
        compiler_params=params,
        name="products_other",
    )(side, other_part, other_b, narrow_b, *markers_info, gram, products)

    gram = gram + exchange(gram, 1)
    rest = flips
    while rest:
        if len(rest) > 1:
            near, far, both = (exchange(gram, f | 1) for f in (rest[0], rest[1], rest[0] | rest[1]))
            gram = (gram + near) + (far + both)
        else:
            gram = gram + exchange(gram, rest[0] | 1)
        rest = rest[2:]
    gram = gram[:, : (probes + 1) * BINS].reshape(BINS, probes + 1, BINS)
    return (products.transpose(1, 0, 2), gram.transpose(0, 2, 1))


def solution(mesh):
    in_specs = (
        P(("grp", "samp"), None),
        P(None, ("grp", "samp")),
        P(("grp", "samp")),
        P(),
        P(),
        P(),
    )
    out_specs = (P(None, None, ("grp", "samp")), P("grp", None, None))
    return jax.shard_map(shards, mesh=mesh, in_specs=in_specs, out_specs=out_specs, check_vma=False)
```

```python
import functools

import jax
import jax.numpy as jnp
from jax import lax
from jax.experimental import pallas as pl
from jax.experimental.pallas import tpu as pltpu
from jax.sharding import PartitionSpec as P

BINS = 16
LANES = 128
GROUP = LANES // BINS
F32 = jnp.float32
BF16 = jnp.bfloat16
MIB = 2**20
PIECES = 2

dot_nt = functools.partial(lax.dot_general, dimension_numbers=(((1,), (1,)), ((), ())), preferred_element_type=F32)


def two_parts(x):
    hi = x.astype(BF16)
    return hi, (x - hi.astype(F32)).astype(BF16)


def sign_rows(signs_ref):
    return (2 * signs_ref[...] - 1).astype(F32).astype(BF16)


def pheno_rows(pheno_ref):
    pheno = pheno_ref[...]
    high = pheno.astype(BF16).astype(F32)
    rest = pheno - high
    middle = rest.astype(BF16).astype(F32)
    tail = jnp.zeros((13, pheno.shape[1]), F32)
    return jnp.concatenate([high, middle, rest - middle, tail], axis=0).astype(BF16)


def add_three(x):
    return x[:1] + x[1:2] + x[2:3]


def accumulate(vectors, geno_hbm, narrow_ref, raw, acc, sems, start, chunk):
    samples, markers = raw.shape
    rows = [slice(c * chunk, (c + 1) * chunk) for c in range(samples // chunk)]
    copies = [pltpu.make_async_copy(geno_hbm.at[s, start : start + markers], raw.at[s], sems.at[c]) for c, s in enumerate(rows)]
    for copy in copies:
        copy.start()
    yield
    for c, s in enumerate(rows):
        copies[c].wait()
        narrow = raw[s].astype(F32).astype(BF16)
        narrow_ref[s] = narrow
        part = jnp.dot(vectors()[:, s], narrow, preferred_element_type=F32)
        if c == 0:
            acc[...] = part
        else:
            acc[...] += part
    yield


def place_rows(side, acc, sums, own_ref, other_ref, at):
    half, _ = own_ref.shape
    markers = acc.shape[1]
    for ref, which in ((own_ref, side), (other_ref, 1 - side)):
        ref[:, :markers] = acc[pl.ds(pl.multiple_of(which * half, half), half), :]
        ref[:, at:] = jnp.zeros((half, LANES), F32)
        ref[:1, at : at + half] = jnp.where(which == 0, sums[:, :half], sums[:, half : 2 * half])


def first_sums_kernel(side_ref, geno_hbm, signs_ref, own_ref, other_ref, narrow_ref, raw, acc, sems, *, start, chunk):
    vectors = None
    steps = accumulate(lambda: vectors, geno_hbm, narrow_ref, raw, acc, sems, start, chunk)
    next(steps)
    vectors = sign_rows(signs_ref)
    sums = dot_nt(jnp.ones((8, vectors.shape[1]), BF16), vectors)[:1]
    next(steps)
    place_rows(side_ref[0], acc, sums, own_ref, other_ref, raw.shape[1])


def second_sums_kernel(side_ref, geno_hbm, signs_ref, pheno_ref, first_ref, own_ref, other_ref, narrow_ref, raw, acc, sems, *, start, chunk):
    markers = raw.shape[1]
    probes = signs_ref.shape[0]
    vectors = None
    steps = accumulate(lambda: vectors, geno_hbm, narrow_ref, raw, acc, sems, start, chunk)
    next(steps)
    pheno = pheno_rows(pheno_ref)
    vectors = jnp.concatenate([sign_rows(signs_ref), pheno], axis=0)
    sums = dot_nt(jnp.ones((8, vectors.shape[1]), BF16), vectors)[:1]
    first = add_three(jnp.dot(pheno, first_ref[...], preferred_element_type=F32)[:8])
    next(steps)
    place_rows(side_ref[0], acc, sums, own_ref, other_ref, markers + LANES)
    half = own_ref.shape[0]
    last = sums[:, probes : probes + 1] + sums[:, probes + 1 : probes + 2] + sums[:, probes + 2 : probes + 3]
    row = jnp.concatenate([first, add_three(acc[probes : probes + 8, :])], axis=1)
    for ref in (own_ref, other_ref):
        ref[:1, markers + LANES + half : markers + LANES + half + 1] = last
        for t in range(row.shape[1] // LANES):
            ref[t : t + 1, markers : markers + LANES] = row[:, t * LANES : (t + 1) * LANES]


class Half:
    def __init__(self, mean_ref, scale_ref, bin_ref, geno_ref, start, norm):
        markers = geno_ref.shape[1]
        self.geno = geno_ref
        self.mean = mean_ref[:, start : start + markers]
        scale = scale_ref[:, start : start + markers]
        self.scale = scale * scale * norm
        self.member = (bin_ref[:, start : start + markers] == lax.broadcasted_iota(jnp.int32, (BINS, markers), 0)).astype(F32)

    def scores(self, sums, total):
        return (sums - self.mean * total) * self.scale

    def probe_scores(self, ref):
        markers = self.mean.shape[1]
        at = ref.shape[1] - LANES
        return [self.scores(ref[r : r + 1, :markers], ref[:1, at + r : at + r + 1]) for r in range(ref.shape[0])]

    def weigh(self, rows, weights):
        shifts = []
        count = len(rows) * BINS
        for r, row in enumerate(rows):
            weighted = self.member * row
            shifts.append(jnp.sum(weighted * self.mean, axis=1, keepdims=True))
            hi, lo = two_parts(weighted)
            weights[r * BINS : (r + 1) * BINS, :] = hi
            weights[count + r * BINS : count + (r + 1) * BINS, :] = lo
        return jnp.concatenate(shifts, axis=0)

    def multiply(self, weights, span=slice(None)):
        both = dot_nt(weights[...], self.geno[span, :])
        count = both.shape[0] // 2
        return both[:count] + both[count:]

    def products(self, rows, weights):
        shift = self.weigh(rows, weights)
        return self.multiply(weights) - shift


def square_of(products):
    count = products.shape[0]
    hi, lo = two_parts(products)
    both = dot_nt(jnp.concatenate([hi, lo], axis=0), hi)
    return both[:count] + (both[count:] + both[count:].T)


def gram_of(products, gram_norm):
    column = lax.broadcasted_iota(jnp.int32, (BINS, LANES), 1)
    parts = []
    for g in range(products.shape[0] // LANES):
        square = square_of(products[g * LANES : (g + 1) * LANES])
        total = square[:BINS]
        for r in range(1, GROUP):
            total = jnp.where(column // BINS == r, square[r * BINS : (r + 1) * BINS], total)
        parts.append(total * gram_norm)
    h = BINS // 2
    packed = []
    for one, two in zip(parts[::2], parts[1::2]):
        moved = pltpu.roll(two[h:], LANES - h, 1)
        packed += [one[:h], two[:h], jnp.where(column[:h] % BINS >= h, one[h:], moved)]
    return jnp.concatenate(packed, axis=1)


def unpack_kernel(one_ref, two_ref, out_ref, upper, lower, *, pairs):
    h = BINS // 2
    count = upper.shape[0] // BINS
    packed = one_ref[...] + two_ref[...]
    tile = [packed[:, t * LANES : (t + 1) * LANES] for t in range(packed.shape[1] // LANES)]
    for p in range(pairs):
        one, two, low = tile[3 * p : 3 * p + 3]
        for i, (a, b) in enumerate(((one, low), (two, pltpu.roll(low, h, 1)))):
            at = (2 * p + i) * LANES
            upper[at : at + LANES, :] = a.T
            lower[at : at + LANES, :] = b.T
    last = tile[3 * pairs].T
    upper[2 * pairs * LANES :, :] = last[:BINS]
    lower[2 * pairs * LANES :, :] = last[BINS : 2 * BINS]
    for l in range(BINS):
        row = upper[pl.ds(l, count, stride=BINS), :].T
        out_ref[:h, l, :] = row
        if l >= h:
            out_ref[l, :h, :] = row
            out_ref[h:, l, :] = lower[pl.ds(l, count, stride=BINS), :].T


def part_kernel(own_a, geno_a, mean_ref, scale_ref, bin_ref, part_ref, weights, *, norm):
    first = Half(mean_ref, scale_ref, bin_ref, geno_a, 0, norm)
    part_ref[...] = first.products(first.probe_scores(own_a), weights)


def own_kernel(side_ref, part_ref, other_a, own_b, geno_a, geno_b, mean_ref, scale_ref, bin_ref, out_ref, gram_ref, other_ref, last_ref, weights, prod, sems, *, norm, gram_norm):
    half = own_b.shape[0]
    count = half * BINS
    markers = geno_a.shape[1]
    samples = geno_a.shape[0]
    first = Half(mean_ref, scale_ref, bin_ref, geno_a, 0, norm)
    second = Half(mean_ref, scale_ref, bin_ref, geno_b, markers, norm)
    tiles = markers // LANES
    pheno = [own_b[t : t + 1, markers : markers + LANES] for t in range(2 * tiles)]
    total = own_b[:1, markers + LANES + half : markers + LANES + half + 1]
    rows_b = second.probe_scores(own_b) + [second.scores(jnp.concatenate(pheno[tiles:], axis=1), total)]
    rows_a = first.probe_scores(other_a) + [first.scores(jnp.concatenate(pheno[:tiles], axis=1), total)]
    parts_b = second.products(rows_b, weights.at[0])
    mine = part_ref[...] + parts_b[:count]
    prod[...] = mine.reshape(half, BINS, samples)
    copy = pltpu.make_async_copy(prod, out_ref.at[pl.ds(pl.multiple_of(side_ref[0] * half, half), half)], sems.at[0])
    copy.start()
    probe_gram = gram_of(mine, gram_norm)
    gram_ref[:, : probe_gram.shape[1]] = probe_gram
    parts_a = first.products(rows_a, weights.at[1])
    other_ref[...] = parts_a[:count]
    last = parts_a[count:] + parts_b[count:]
    last_ref[0] = last
    square = square_of(last) * gram_norm
    h = BINS // 2
    rest = jnp.zeros((h, LANES - 2 * BINS), F32)
    gram_ref[:, probe_gram.shape[1] :] = jnp.concatenate([square[:h], square[h:], rest], axis=1)
    copy.wait()


def other_kernel(side_ref, part_ref, last_ref, other_b, geno_b, mean_ref, scale_ref, bin_ref, own_gram_ref, _, out_ref, gram_ref, weights, prod, sems, *, norm, gram_norm):
    half = other_b.shape[0]
    wide = half * BINS
    samples, markers = geno_b.shape
    side = side_ref[0]
    copies = [pltpu.make_async_copy(last_ref, out_ref.at[pl.ds(2 * half, 1)], sems.at[0])]
    copies[0].start()
    second = Half(mean_ref, scale_ref, bin_ref, geno_b, markers, norm)
    shift = second.weigh(second.probe_scores(other_b), weights)
    pieces = sems.shape[0] - 1
    width = samples // pieces
    for p in range(pieces):
        span = slice(p * width, (p + 1) * width)
        products = part_ref[:, span] + (second.multiply(weights, span) - shift)
        prod[:, :, span] = products.reshape(half, BINS, width)
        to = out_ref.at[pl.ds(pl.multiple_of((1 - side) * half, half), half), :, span]
        copies.append(pltpu.make_async_copy(prod.at[:, :, span], to, sems.at[p + 1]))
        copies[-1].start()
    gram = gram_of(prod[...].reshape(wide, samples), gram_norm)
    packed = gram.shape[1]
    gram_ref[:, pl.ds(pl.multiple_of((1 - side) * packed, packed), packed)] = gram
    gram_ref[:, pl.ds(pl.multiple_of(side * packed, packed), packed)] = own_gram_ref[:, :packed]
    gram_ref[:, 2 * packed :] = own_gram_ref[:, packed:]
    for copy in copies:
        copy.wait()


def parity(i):
    return bin(i).count("1") % 2


def exchange(x, even, odd=None):
    pairs = [(i, i ^ (even if odd is None or not parity(i) else odd)) for i in range(lax.axis_size("samp"))]
    return lax.ppermute(x, "samp", pairs)


def shards(genotypes, probe_signs, phenotype, marker_mean, marker_scale, marker_bin):
    samples, markers = genotypes.shape
    probes = probe_signs.shape[0]
    half = probes // 2
    devices = lax.axis_size("samp")
    total = samples * devices
    side = (lax.population_count(lax.axis_index("samp")) & 1).astype(jnp.int32).reshape(1)
    markers_info = [x.reshape(1, markers) for x in (marker_mean, marker_scale, marker_bin)]
    pheno = phenotype.reshape(1, samples)
    smem = pl.BlockSpec(memory_space=pltpu.SMEM)
    vmem = pl.BlockSpec(memory_space=pltpu.VMEM)
    hbm = pl.BlockSpec(memory_space=pl.ANY)

    width = markers // 2
    chunk = min(samples, 128)
    narrow = jax.ShapeDtypeStruct((samples, width), BF16)

    def sums(kernel, start, name, extra, rows, *operands):
        part = jax.ShapeDtypeStruct((half, width + extra), F32)
        return pl.pallas_call(
            functools.partial(kernel, start=start, chunk=chunk),
            out_shape=(part, part, narrow),
            in_specs=[smem, hbm] + [vmem] * (len(operands) - 2),
            out_specs=(vmem, vmem, vmem),
            scratch_shapes=[
                pltpu.VMEM((samples, width), jnp.int32),
                pltpu.VMEM((rows, width), F32),
                pltpu.SemaphoreType.DMA((samples // chunk,)),
            ],
            cost_estimate=pl.CostEstimate(flops=2 * rows * samples * width, bytes_accessed=6 * samples * width, transcendentals=0),
            compiler_params=pltpu.CompilerParams(vmem_limit_bytes=47 * MIB),
            name=name,
        )(*operands)

    flips = [1 << b for b in range(1, devices.bit_length() - 1)]
    own_a, other_a, narrow_a = sums(first_sums_kernel, 0, "sums_first", LANES, probes, side, genotypes, probe_signs)
    own_b, other_b, narrow_b = sums(
        second_sums_kernel, width, "sums_second", 2 * LANES, probes + 16, side, genotypes, probe_signs, pheno, narrow_a
    )
    own_a = own_a + exchange(other_a, 1)
    own_b = own_b + exchange(other_b, 1)
    swapped = flips[1:2] + flips[:1] + flips[2:]
    received = None
    for a_even, a_odd, b_even, b_odd in zip(flips, flips[1:] + flips[:1], swapped, flips[::-1]):
        own_a = own_a + exchange(own_a, a_even | 1, a_odd | 1)
        if received is not None:
            own_b = own_b + received
        received = exchange(own_b, b_even | 1, b_odd | 1)

    norm = (total * (markers // BINS)) ** -0.5
    gram_norm = 1.0 / total
    rows = half * BINS
    packed = rows // LANES * 3 * LANES // 2

    def work(count):
        return pl.CostEstimate(flops=4 * count * samples * width, bytes_accessed=4 * rows * samples, transcendentals=0)

    params = pltpu.CompilerParams(vmem_limit_bytes=32 * MIB)
    part = jax.ShapeDtypeStruct((rows, samples), F32)
    weights = pltpu.VMEM((2 * rows, width), BF16)
    products = jax.ShapeDtypeStruct((probes + 1, BINS, samples), F32)

    other_a = exchange(own_a, 1)
    own_part = pl.pallas_call(
        functools.partial(part_kernel, norm=norm),
        out_shape=part,
        in_specs=[vmem] * 5,
        out_specs=vmem,
        scratch_shapes=[weights],
        cost_estimate=work(rows),
        compiler_params=params,
        name="products_part",
    )(own_a, narrow_a, *markers_info)
    own_b, received, own_part = lax.optimization_barrier((own_b, received, own_part))
    own_b = own_b + received
    other_b = exchange(own_b, 1)
    products, gram, other_part, last = pl.pallas_call(
        functools.partial(own_kernel, norm=norm, gram_norm=gram_norm),
        out_shape=(products, jax.ShapeDtypeStruct((BINS // 2, packed + LANES), F32), part, jax.ShapeDtypeStruct((1, BINS, samples), F32)),
        in_specs=[smem] + [vmem] * 8,
        out_specs=(hbm, vmem, vmem, vmem),
        scratch_shapes=[
            pltpu.VMEM((2, 2 * (rows + BINS), width), BF16),
            pltpu.VMEM((half, BINS, samples), F32),
            pltpu.SemaphoreType.DMA((1,)),
        ],
        cost_estimate=work(2 * rows),
        compiler_params=params,
        name="products_own",
    )(side, own_part, other_a, own_b, narrow_a, narrow_b, *markers_info)
    products, gram = pl.pallas_call(
        functools.partial(other_kernel, norm=norm, gram_norm=gram_norm),
        out_shape=(products, jax.ShapeDtypeStruct((BINS // 2, 2 * packed + LANES), F32)),
        in_specs=[smem] + [vmem] * 8 + [hbm],
        out_specs=(hbm, vmem),
        scratch_shapes=[weights, pltpu.VMEM((half, BINS, samples), F32), pltpu.SemaphoreType.DMA((PIECES + 1,))],
        input_output_aliases={9: 0},
        cost_estimate=work(rows),
        compiler_params=params,
        name="products_other",
    )(side, other_part, last, other_b, narrow_b, *markers_info, gram, products)

    gram = gram + exchange(gram, 1)
    rest = flips
    while len(rest) > 1:
        near, far, both = (exchange(gram, f | 1) for f in (rest[0], rest[1], rest[0] | rest[1]))
        gram = (gram + near) + (far + both)
        rest = rest[2:]
    last = exchange(gram, rest[0] | 1) if rest else jnp.zeros_like(gram)
    count = (probes + 1) * BINS
    gram = pl.pallas_call(
        functools.partial(unpack_kernel, pairs=2 * rows // (2 * LANES)),
        out_shape=jax.ShapeDtypeStruct((BINS, BINS, probes + 1), F32),
        in_specs=[vmem, vmem],
        out_specs=vmem,
        scratch_shapes=[pltpu.VMEM((count, BINS // 2), F32), pltpu.VMEM((count, BINS // 2), F32)],
        compiler_params=pltpu.CompilerParams(vmem_limit_bytes=16 * MIB),
        name="gram_unpack",
    )(gram, last)
    return (products.transpose(1, 0, 2), gram)


def solution(mesh):
    in_specs = (
        P(("grp", "samp"), None),
        P(None, ("grp", "samp")),
        P(("grp", "samp")),
        P(),
        P(),
        P(),
    )
    out_specs = (P(None, None, ("grp", "samp")), P("grp", None, None))
    return jax.shard_map(shards, mesh=mesh, in_specs=in_specs, out_specs=out_specs, check_vma=False)
```

```python
import functools

import jax
import jax.numpy as jnp
from jax import lax
from jax.experimental import pallas as pl
from jax.experimental.pallas import tpu as pltpu
from jax.sharding import PartitionSpec as P

BINS = 16
LANES = 128
GROUP = LANES // BINS
F32 = jnp.float32
BF16 = jnp.bfloat16
MIB = 2**20

dot_nt = functools.partial(lax.dot_general, dimension_numbers=(((1,), (1,)), ((), ())), preferred_element_type=F32)


def two_parts(x):
    hi = x.astype(BF16)
    return hi, (x - hi.astype(F32)).astype(BF16)


def sign_rows(signs_ref):
    return (2 * signs_ref[...] - 1).astype(F32).astype(BF16)


def pheno_rows(pheno_ref):
    pheno = pheno_ref[...]
    high = pheno.astype(BF16).astype(F32)
    rest = pheno - high
    middle = rest.astype(BF16).astype(F32)
    tail = jnp.zeros((13, pheno.shape[1]), F32)
    return jnp.concatenate([high, middle, rest - middle, tail], axis=0).astype(BF16)


def add_three(x):
    return x[:1] + x[1:2] + x[2:3]


def narrowed(geno_hbm, narrow_ref, raw, sems, start, chunk):
    samples, markers = raw.shape
    rows = [slice(c * chunk, (c + 1) * chunk) for c in range(samples // chunk)]
    copies = [pltpu.make_async_copy(geno_hbm.at[s, start : start + markers], raw.at[s], sems.at[c]) for c, s in enumerate(rows)]
    for copy in copies:
        copy.start()

    def finish():
        for copy, s in zip(copies, rows):
            copy.wait()
            narrow = raw[s].astype(F32).astype(BF16)
            narrow_ref[s] = narrow
            yield s, narrow

    return finish


def place_rows(side, vectors, acc, own_ref, other_ref):
    half = own_ref.shape[0]
    probes = 2 * half
    markers = acc.shape[1]
    tiles = markers // LANES
    sums = dot_nt(jnp.ones((8, vectors.shape[1]), BF16), vectors)[:1]
    last = sums[:, probes : probes + 1] + sums[:, probes + 1 : probes + 2] + sums[:, probes + 2 : probes + 3]
    pheno = add_three(acc[probes : probes + 8, :])
    for ref, which in ((own_ref, side), (other_ref, 1 - side)):
        ref[:, :markers] = acc[pl.ds(pl.multiple_of(which * half, half), half), :]
        ref[: half - tiles, markers:] = jnp.zeros((half - tiles, LANES), F32)
        ref[:1, markers : markers + half] = jnp.where(which == 0, sums[:, :half], sums[:, half:probes])
        ref[:1, markers + half : markers + half + 1] = last
        for t in range(tiles):
            ref[half - tiles + t : half - tiles + t + 1, markers:] = pheno[:, t * LANES : (t + 1) * LANES]


def vector_rows(signs_ref, pheno_ref):
    return jnp.concatenate([sign_rows(signs_ref), pheno_rows(pheno_ref)], axis=0)


def narrow_kernel(geno_hbm, narrow_ref, raw, sems, *, start, chunk):
    for _ in narrowed(geno_hbm, narrow_ref, raw, sems, start, chunk)():
        pass


def first_sums_kernel(side_ref, narrow_ref, signs_ref, pheno_ref, own_ref, other_ref, acc):
    vectors = vector_rows(signs_ref, pheno_ref)
    acc[...] = jnp.dot(vectors, narrow_ref[...], preferred_element_type=F32)
    place_rows(side_ref[0], vectors, acc, own_ref, other_ref)


def second_sums_kernel(side_ref, geno_hbm, signs_ref, pheno_ref, own_ref, other_ref, narrow_ref, raw, acc, sems, *, start, chunk):
    finish = narrowed(geno_hbm, narrow_ref, raw, sems, start, chunk)
    vectors = vector_rows(signs_ref, pheno_ref)
    for s, narrow in finish():
        part = jnp.dot(vectors[:, s], narrow, preferred_element_type=F32)
        if s.start == 0:
            acc[...] = part
        else:
            acc[...] += part
    place_rows(side_ref[0], vectors, acc, own_ref, other_ref)


class Half:
    def __init__(self, mean_ref, scale_ref, bin_ref, geno_ref, start, norm):
        markers = geno_ref.shape[1]
        self.geno = geno_ref
        self.mean = mean_ref[:, start : start + markers]
        scale = scale_ref[:, start : start + markers]
        self.scale = scale * scale * norm
        self.member = (bin_ref[:, start : start + markers] == lax.broadcasted_iota(jnp.int32, (BINS, markers), 0)).astype(F32)

    def scores(self, sums, total):
        return (sums - self.mean * total) * self.scale

    def probe_scores(self, ref):
        markers = self.mean.shape[1]
        return [self.scores(ref[r : r + 1, :markers], ref[:1, markers + r : markers + r + 1]) for r in range(ref.shape[0])]

    def pheno_scores(self, ref):
        half = ref.shape[0]
        markers = self.mean.shape[1]
        tiles = markers // LANES
        row = jnp.concatenate([ref[t : t + 1, markers:] for t in range(half - tiles, half)], axis=1)
        return self.scores(row, ref[:1, markers + half : markers + half + 1])

    def weigh(self, rows, weights):
        shifts = []
        count = len(rows) * BINS
        for r, row in enumerate(rows):
            weighted = self.member * row
            shifts.append(jnp.sum(weighted * self.mean, axis=1, keepdims=True))
            hi, lo = two_parts(weighted)
            weights[r * BINS : (r + 1) * BINS, :] = hi
            weights[count + r * BINS : count + (r + 1) * BINS, :] = lo
        return jnp.concatenate(shifts, axis=0)

    def multiply(self, weights, span=slice(None)):
        both = dot_nt(weights[...], self.geno[span, :])
        count = both.shape[0] // 2
        return both[:count] + both[count:]

    def products(self, rows, weights):
        shift = self.weigh(rows, weights)
        return self.multiply(weights) - shift


def square_of(products):
    count = products.shape[0]
    hi, lo = two_parts(products)
    both = dot_nt(jnp.concatenate([hi, lo], axis=0), hi)
    return both[:count] + (both[count:] + both[count:].T)


def gram_of(products, gram_norm):
    column = lax.broadcasted_iota(jnp.int32, (BINS, LANES), 1)
    parts = []
    for g in range(products.shape[0] // LANES):
        square = square_of(products[g * LANES : (g + 1) * LANES])
        total = square[:BINS]
        for r in range(1, GROUP):
            total = jnp.where(column // BINS == r, square[r * BINS : (r + 1) * BINS], total)
        parts.append(total * gram_norm)
    h = BINS // 2
    packed = []
    for one, two in zip(parts[::2], parts[1::2]):
        moved = pltpu.roll(two[h:], LANES - h, 1)
        packed += [one[:h], two[:h], jnp.where(column[:h] % BINS >= h, one[h:], moved)]
    return jnp.concatenate(packed, axis=1)


def unpack_kernel(one_ref, two_ref, out_ref, upper, lower, *, pairs):
    h = BINS // 2
    count = upper.shape[0] // BINS
    packed = one_ref[...] + two_ref[...]
    tile = [packed[:, t * LANES : (t + 1) * LANES] for t in range(packed.shape[1] // LANES)]
    for p in range(pairs):
        one, two, low = tile[3 * p : 3 * p + 3]
        for i, (a, b) in enumerate(((one, low), (two, pltpu.roll(low, h, 1)))):
            at = (2 * p + i) * LANES
            upper[at : at + LANES, :] = a.T
            lower[at : at + LANES, :] = b.T
    last = tile[3 * pairs].T
    upper[2 * pairs * LANES :, :] = last[:BINS]
    lower[2 * pairs * LANES :, :] = last[BINS : 2 * BINS]
    for l in range(BINS):
        row = upper[pl.ds(l, count, stride=BINS), :].T
        out_ref[:h, l, :] = row
        if l >= h:
            out_ref[l, :h, :] = row
            out_ref[h:, l, :] = lower[pl.ds(l, count, stride=BINS), :].T


def part_kernel(sums_a, geno_a, mean_ref, scale_ref, bin_ref, part_ref, weights, *, norm, pheno):
    first = Half(mean_ref, scale_ref, bin_ref, geno_a, 0, norm)
    rows = first.probe_scores(sums_a) + ([first.pheno_scores(sums_a)] if pheno else [])
    part_ref[...] = first.products(rows, weights)


def own_kernel(own_part, other_part, own_b, geno_b, mean_ref, scale_ref, bin_ref, mine_ref, last_ref, gram_ref, weights, *, norm, gram_norm):
    half = own_b.shape[0]
    count = half * BINS
    samples, markers = geno_b.shape
    second = Half(mean_ref, scale_ref, bin_ref, geno_b, markers, norm)
    parts = second.products(second.probe_scores(own_b) + [second.pheno_scores(own_b)], weights)
    mine = own_part[...] + parts[:count]
    mine_ref[...] = mine.reshape(half, BINS, samples)
    last = other_part[count:] + parts[count:]
    last_ref[0] = last
    probe_gram = gram_of(mine, gram_norm)
    gram_ref[:, : probe_gram.shape[1]] = probe_gram
    square = square_of(last) * gram_norm
    h = BINS // 2
    rest = jnp.zeros((h, LANES - 2 * BINS), F32)
    gram_ref[:, probe_gram.shape[1] :] = jnp.concatenate([square[:h], square[h:], rest], axis=1)


def other_kernel(side_ref, part_ref, other_b, geno_b, mean_ref, scale_ref, bin_ref, own_gram_ref, theirs_ref, gram_ref, weights, *, norm, gram_norm):
    half = other_b.shape[0]
    side = side_ref[0]
    samples, markers = geno_b.shape
    second = Half(mean_ref, scale_ref, bin_ref, geno_b, markers, norm)
    products = part_ref[: half * BINS] + second.products(second.probe_scores(other_b), weights)
    theirs_ref[...] = products.reshape(half, BINS, samples)
    gram = gram_of(products, gram_norm)
    packed = gram.shape[1]
    gram_ref[:, pl.ds(pl.multiple_of((1 - side) * packed, packed), packed)] = gram
    gram_ref[:, pl.ds(pl.multiple_of(side * packed, packed), packed)] = own_gram_ref[:, :packed]
    gram_ref[:, 2 * packed :] = own_gram_ref[:, packed:]


def store_kernel(side_ref, mine_ref, theirs_ref, last_ref, out_ref, sems):
    half = mine_ref.shape[0]
    copies = []
    for i, (ref, which) in enumerate(((mine_ref, side_ref[0]), (theirs_ref, 1 - side_ref[0]))):
        to = out_ref.at[pl.ds(pl.multiple_of(which * half, half), half)]
        copies.append(pltpu.make_async_copy(ref, to, sems.at[i]))
    copies.append(pltpu.make_async_copy(last_ref, out_ref.at[pl.ds(2 * half, 1)], sems.at[2]))
    for copy in copies:
        copy.start()
    for copy in copies:
        copy.wait()


def parity(i):
    return bin(i).count("1") % 2


def exchange(x, even, odd=None):
    pairs = [(i, i ^ (even if odd is None or not parity(i) else odd)) for i in range(lax.axis_size("samp"))]
    return lax.ppermute(x, "samp", pairs)


def shards(genotypes, probe_signs, phenotype, marker_mean, marker_scale, marker_bin):
    samples, markers = genotypes.shape
    probes = probe_signs.shape[0]
    half = probes // 2
    devices = lax.axis_size("samp")
    total = samples * devices
    side = (lax.population_count(lax.axis_index("samp")) & 1).astype(jnp.int32).reshape(1)
    markers_info = [x.reshape(1, markers) for x in (marker_mean, marker_scale, marker_bin)]
    pheno = phenotype.reshape(1, samples)
    smem = pl.BlockSpec(memory_space=pltpu.SMEM)
    vmem = pl.BlockSpec(memory_space=pltpu.VMEM)
    hbm = pl.BlockSpec(memory_space=pl.ANY)

    width = markers // 2
    chunk = min(samples, 128)
    narrow = jax.ShapeDtypeStruct((samples, width), BF16)

    part = jax.ShapeDtypeStruct((half, width + LANES), F32)
    raw = [pltpu.VMEM((samples, width), jnp.int32)]
    acc = [pltpu.VMEM((probes + 16, width), F32)]
    sems = [pltpu.SemaphoreType.DMA((samples // chunk,))]

    def local(kernel, name, out_shape, scratch, work, moved, mib, *operands, **options):
        spaces = {id(side): smem, id(genotypes): hbm}
        return pl.pallas_call(
            functools.partial(kernel, **options),
            out_shape=out_shape,
            in_specs=[spaces.get(id(x), vmem) for x in operands],
            out_specs=jax.tree.map(lambda _: vmem, out_shape),
            scratch_shapes=scratch,
            cost_estimate=pl.CostEstimate(flops=2 * work * samples * width, bytes_accessed=moved, transcendentals=0),
            compiler_params=pltpu.CompilerParams(vmem_limit_bytes=mib * MIB),
            name=name,
        )(*operands)

    flips = [1 << b for b in range(1, devices.bit_length() - 1)]
    large = 6 * samples * width
    narrow_a = local(narrow_kernel, "narrow_first", narrow, raw + sems, 0, large, 47, genotypes, start=0, chunk=chunk)
    own_a, other_a = local(
        first_sums_kernel, "sums_first", (part, part), acc, probes, 2 * samples * width, 32, side, narrow_a, probe_signs, pheno
    )
    own_b, other_b, narrow_b = local(
        second_sums_kernel,
        "sums_second",
        (part, part, narrow),
        raw + acc + sems,
        probes,
        large,
        47,
        side,
        genotypes,
        probe_signs,
        pheno,
        start=width,
        chunk=chunk,
    )
    own_a = own_a + exchange(other_a, 1)
    own_b = own_b + exchange(other_b, 1)
    swapped = flips[1:2] + flips[:1] + flips[2:]
    received = None
    for a_even, a_odd, b_even, b_odd in zip(flips, flips[1:] + flips[:1], swapped, flips[::-1]):
        own_a = own_a + exchange(own_a, a_even | 1, a_odd | 1)
        if received is not None:
            own_b = own_b + received
        received = exchange(own_b, b_even | 1, b_odd | 1)

    norm = (total * (markers // BINS)) ** -0.5
    gram_norm = 1.0 / total
    rows = half * BINS
    packed = rows // LANES * 3 * LANES // 2
    probe_rows = jax.ShapeDtypeStruct((half, BINS, samples), F32)

    def multiply(kernel, name, count, out_shape, *operands, **options):
        scratch = [pltpu.VMEM((2 * count, width), BF16)]
        return local(kernel, name, out_shape, scratch, 2 * count, 4 * count * samples, 32, *operands, norm=norm, **options)

    other_a = exchange(own_a, 1)
    own_part, other_part = (
        multiply(part_kernel, name, count, jax.ShapeDtypeStruct((count, samples), F32), x, narrow_a, *markers_info, pheno=count > rows)
        for name, count, x in (("products_part", rows, own_a), ("products_part_other", rows + BINS, other_a))
    )
    own_b, received, other_part = lax.optimization_barrier((own_b, received, other_part))
    own_b = own_b + received
    other_b = exchange(own_b, 1)
    out_shape = (
        probe_rows,
        jax.ShapeDtypeStruct((1, BINS, samples), F32),
        jax.ShapeDtypeStruct((BINS // 2, packed + LANES), F32),
    )
    mine, last, gram = multiply(
        own_kernel, "products_own", rows + BINS, out_shape, own_part, other_part, own_b, narrow_b, *markers_info, gram_norm=gram_norm
    )
    out_shape = (probe_rows, jax.ShapeDtypeStruct((BINS // 2, 2 * packed + LANES), F32))
    theirs, gram = multiply(
        other_kernel, "products_other", rows, out_shape, side, other_part, other_b, narrow_b, *markers_info, gram, gram_norm=gram_norm
    )
    products = pl.pallas_call(
        store_kernel,
        out_shape=jax.ShapeDtypeStruct((probes + 1, BINS, samples), F32),
        in_specs=[smem, vmem, vmem, vmem],
        out_specs=hbm,
        scratch_shapes=[pltpu.SemaphoreType.DMA((3,))],
        cost_estimate=pl.CostEstimate(flops=0, bytes_accessed=4 * (probes + 1) * BINS * samples, transcendentals=0),
        compiler_params=pltpu.CompilerParams(vmem_limit_bytes=16 * MIB),
        name="products_store",
    )(side, mine, theirs, last)

    gram = gram + exchange(gram, 1)
    rest = flips
    while len(rest) > 1:
        near, far, both = (exchange(gram, f | 1) for f in (rest[0], rest[1], rest[0] | rest[1]))
        gram = (gram + near) + (far + both)
        rest = rest[2:]
    last = exchange(gram, rest[0] | 1) if rest else jnp.zeros_like(gram)
    count = (probes + 1) * BINS
    gram = pl.pallas_call(
        functools.partial(unpack_kernel, pairs=2 * rows // (2 * LANES)),
        out_shape=jax.ShapeDtypeStruct((BINS, BINS, probes + 1), F32),
        in_specs=[vmem, vmem],
        out_specs=vmem,
        scratch_shapes=[pltpu.VMEM((count, BINS // 2), F32), pltpu.VMEM((count, BINS // 2), F32)],
        compiler_params=pltpu.CompilerParams(vmem_limit_bytes=16 * MIB),
        name="gram_unpack",
    )(gram, last)
    return (products.transpose(1, 0, 2), gram)


def solution(mesh):
    in_specs = (
        P(("grp", "samp"), None),
        P(None, ("grp", "samp")),
        P(("grp", "samp")),
        P(),
        P(),
        P(),
    )
    out_specs = (P(None, None, ("grp", "samp")), P("grp", None, None))
    return jax.shard_map(shards, mesh=mesh, in_specs=in_specs, out_specs=out_specs, check_vma=False)
```

```python
import functools

import jax
import jax.numpy as jnp
from jax import lax
from jax.experimental import pallas as pl
from jax.experimental.pallas import tpu as pltpu
from jax.sharding import PartitionSpec as P

BINS = 16
LANES = 128
GROUP = LANES // BINS
F32 = jnp.float32
BF16 = jnp.bfloat16
MIB = 2**20

dot_nt = functools.partial(lax.dot_general, dimension_numbers=(((1,), (1,)), ((), ())), preferred_element_type=F32)


def two_parts(x):
    hi = x.astype(BF16)
    return hi, (x - hi.astype(F32)).astype(BF16)


def sign_rows(signs_ref):
    return (2 * signs_ref[...] - 1).astype(F32).astype(BF16)


def pheno_rows(pheno_ref):
    pheno = pheno_ref[...]
    high = pheno.astype(BF16).astype(F32)
    rest = pheno - high
    middle = rest.astype(BF16).astype(F32)
    tail = jnp.zeros((13, pheno.shape[1]), F32)
    return jnp.concatenate([high, middle, rest - middle, tail], axis=0).astype(BF16)


def add_three(x):
    return x[:1] + x[1:2] + x[2:3]


def narrowed(geno_hbm, narrow_ref, raw, sems, start, chunk):
    samples, markers = raw.shape
    rows = [slice(c * chunk, (c + 1) * chunk) for c in range(samples // chunk)]
    copies = [pltpu.make_async_copy(geno_hbm.at[s, start : start + markers], raw.at[s], sems.at[c]) for c, s in enumerate(rows)]
    for copy in copies:
        copy.start()

    def finish():
        for copy, s in zip(copies, rows):
            copy.wait()
            narrow = raw[s].astype(F32).astype(BF16)
            narrow_ref[s] = narrow
            yield s, narrow

    return finish


def place_rows(side, vectors, acc, own_ref, other_ref):
    half = own_ref.shape[0]
    probes = 2 * half
    markers = acc.shape[1]
    tiles = markers // LANES
    sums = dot_nt(jnp.ones((8, vectors.shape[1]), BF16), vectors)[:1]
    last = sums[:, probes : probes + 1] + sums[:, probes + 1 : probes + 2] + sums[:, probes + 2 : probes + 3]
    pheno = add_three(acc[probes : probes + 8, :])
    for ref, which in ((own_ref, side), (other_ref, 1 - side)):
        ref[:, :markers] = acc[pl.ds(pl.multiple_of(which * half, half), half), :]
        ref[: half - tiles, markers:] = jnp.zeros((half - tiles, LANES), F32)
        ref[:1, markers : markers + half] = jnp.where(which == 0, sums[:, :half], sums[:, half:probes])
        ref[:1, markers + half : markers + half + 1] = last
        for t in range(tiles):
            ref[half - tiles + t : half - tiles + t + 1, markers:] = pheno[:, t * LANES : (t + 1) * LANES]


def vector_rows(signs_ref, pheno_ref):
    return jnp.concatenate([sign_rows(signs_ref), pheno_rows(pheno_ref)], axis=0)


def narrow_kernel(geno_hbm, narrow_ref, raw, sems, *, start, chunk):
    for _ in narrowed(geno_hbm, narrow_ref, raw, sems, start, chunk)():
        pass


def first_sums_kernel(side_ref, narrow_ref, signs_ref, pheno_ref, own_ref, other_ref, acc):
    vectors = vector_rows(signs_ref, pheno_ref)
    acc[...] = jnp.dot(vectors, narrow_ref[...], preferred_element_type=F32)
    place_rows(side_ref[0], vectors, acc, own_ref, other_ref)


def second_sums_kernel(side_ref, geno_hbm, signs_ref, pheno_ref, own_ref, other_ref, narrow_ref, raw, acc, sems, *, start, chunk):
    finish = narrowed(geno_hbm, narrow_ref, raw, sems, start, chunk)
    vectors = vector_rows(signs_ref, pheno_ref)
    for s, narrow in finish():
        part = jnp.dot(vectors[:, s], narrow, preferred_element_type=F32)
        if s.start == 0:
            acc[...] = part
        else:
            acc[...] += part
    place_rows(side_ref[0], vectors, acc, own_ref, other_ref)


class Half:
    def __init__(self, mean_ref, scale_ref, bin_ref, geno_ref, start, norm):
        markers = geno_ref.shape[1]
        self.geno = geno_ref
        self.mean = mean_ref[:, start : start + markers]
        scale = scale_ref[:, start : start + markers]
        self.scale = scale * scale * norm
        self.member = (bin_ref[:, start : start + markers] == lax.broadcasted_iota(jnp.int32, (BINS, markers), 0)).astype(F32)

    def scores(self, sums, total):
        return (sums - self.mean * total) * self.scale

    def probe_scores(self, ref):
        markers = self.mean.shape[1]
        return [self.scores(ref[r : r + 1, :markers], ref[:1, markers + r : markers + r + 1]) for r in range(ref.shape[0])]

    def pheno_scores(self, ref):
        half = ref.shape[0]
        markers = self.mean.shape[1]
        tiles = markers // LANES
        row = jnp.concatenate([ref[t : t + 1, markers:] for t in range(half - tiles, half)], axis=1)
        return self.scores(row, ref[:1, markers + half : markers + half + 1])

    def weigh(self, rows, weights):
        shifts = []
        count = len(rows) * BINS
        for r, row in enumerate(rows):
            weighted = self.member * row
            shifts.append(jnp.sum(weighted * self.mean, axis=1, keepdims=True))
            hi, lo = two_parts(weighted)
            weights[r * BINS : (r + 1) * BINS, :] = hi
            weights[count + r * BINS : count + (r + 1) * BINS, :] = lo
        return jnp.concatenate(shifts, axis=0)

    def multiply(self, weights, span=slice(None)):
        both = dot_nt(weights[...], self.geno[span, :])
        count = both.shape[0] // 2
        return both[:count] + both[count:]

    def products(self, rows, weights):
        shift = self.weigh(rows, weights)
        return self.multiply(weights) - shift


def square_of(products):
    count = products.shape[0]
    hi, lo = two_parts(products)
    both = dot_nt(jnp.concatenate([hi, lo], axis=0), hi)
    return both[:count] + (both[count:] + both[count:].T)


def gram_of(products, gram_norm):
    column = lax.broadcasted_iota(jnp.int32, (BINS, LANES), 1)
    parts = []
    for g in range(products.shape[0] // LANES):
        square = square_of(products[g * LANES : (g + 1) * LANES])
        total = square[:BINS]
        for r in range(1, GROUP):
            total = jnp.where(column // BINS == r, square[r * BINS : (r + 1) * BINS], total)
        parts.append(total * gram_norm)
    h = BINS // 2
    packed = []
    for one, two in zip(parts[::2], parts[1::2]):
        moved = pltpu.roll(two[h:], LANES - h, 1)
        packed += [one[:h], two[:h], jnp.where(column[:h] % BINS >= h, one[h:], moved)]
    return jnp.concatenate(packed, axis=1)


def unpack_kernel(one_ref, two_ref, out_ref, upper, lower, *, pairs):
    h = BINS // 2
    count = upper.shape[0] // BINS
    packed = one_ref[...] + two_ref[...]
    tile = [packed[:, t * LANES : (t + 1) * LANES] for t in range(packed.shape[1] // LANES)]
    for p in range(pairs):
        one, two, low = tile[3 * p : 3 * p + 3]
        for i, (a, b) in enumerate(((one, low), (two, pltpu.roll(low, h, 1)))):
            at = (2 * p + i) * LANES
            upper[at : at + LANES, :] = a.T
            lower[at : at + LANES, :] = b.T
    last = tile[3 * pairs].T
    upper[2 * pairs * LANES :, :] = last[:BINS]
    lower[2 * pairs * LANES :, :] = last[BINS : 2 * BINS]
    for l in range(BINS):
        row = upper[pl.ds(l, count, stride=BINS), :].T
        out_ref[:h, l, :] = row
        if l >= h:
            out_ref[l, :h, :] = row
            out_ref[h:, l, :] = lower[pl.ds(l, count, stride=BINS), :].T


def part_kernel(sums_a, geno_a, mean_ref, scale_ref, bin_ref, part_ref, weights, *, norm, pheno):
    first = Half(mean_ref, scale_ref, bin_ref, geno_a, 0, norm)
    rows = first.probe_scores(sums_a) + ([first.pheno_scores(sums_a)] if pheno else [])
    part_ref[...] = first.products(rows, weights)


def own_kernel(own_part, other_part, own_b, geno_b, mean_ref, scale_ref, bin_ref, mine_ref, last_ref, gram_ref, weights, *, norm, gram_norm):
    half = own_b.shape[0]
    count = half * BINS
    samples, markers = geno_b.shape
    second = Half(mean_ref, scale_ref, bin_ref, geno_b, markers, norm)
    parts = second.products(second.probe_scores(own_b) + [second.pheno_scores(own_b)], weights)
    mine = own_part[...] + parts[:count]
    mine_ref[...] = mine.reshape(half, BINS, samples)
    last = other_part[count:] + parts[count:]
    last_ref[0] = last
    probe_gram = gram_of(mine, gram_norm)
    gram_ref[:, : probe_gram.shape[1]] = probe_gram
    square = square_of(last) * gram_norm
    h = BINS // 2
    rest = jnp.zeros((h, LANES - 2 * BINS), F32)
    gram_ref[:, probe_gram.shape[1] :] = jnp.concatenate([square[:h], square[h:], rest], axis=1)


def other_kernel(side_ref, part_ref, other_b, geno_b, mean_ref, scale_ref, bin_ref, own_gram_ref, theirs_ref, gram_ref, weights, *, norm, gram_norm):
    half = other_b.shape[0]
    side = side_ref[0]
    samples, markers = geno_b.shape
    second = Half(mean_ref, scale_ref, bin_ref, geno_b, markers, norm)
    products = part_ref[: half * BINS] + second.products(second.probe_scores(other_b), weights)
    theirs_ref[...] = products.reshape(half, BINS, samples)
    gram = gram_of(products, gram_norm)
    packed = gram.shape[1]
    gram_ref[:, pl.ds(pl.multiple_of((1 - side) * packed, packed), packed)] = gram
    gram_ref[:, pl.ds(pl.multiple_of(side * packed, packed), packed)] = own_gram_ref[:, :packed]
    gram_ref[:, 2 * packed :] = own_gram_ref[:, packed:]


def store_kernel(side_ref, mine_ref, theirs_ref, last_ref, out_ref, sems):
    half = mine_ref.shape[0]
    copies = []
    for i, (ref, which) in enumerate(((mine_ref, side_ref[0]), (theirs_ref, 1 - side_ref[0]))):
        to = out_ref.at[pl.ds(pl.multiple_of(which * half, half), half)]
        copies.append(pltpu.make_async_copy(ref, to, sems.at[i]))
    copies.append(pltpu.make_async_copy(last_ref, out_ref.at[pl.ds(2 * half, 1)], sems.at[2]))
    for copy in copies:
        copy.start()
    for copy in copies:
        copy.wait()


def parity(i):
    return bin(i).count("1") % 2


def exchange(x, even, odd=None):
    pairs = [(i, i ^ (even if odd is None or not parity(i) else odd)) for i in range(lax.axis_size("samp"))]
    return lax.ppermute(x, "samp", pairs)


def shards(genotypes, probe_signs, phenotype, marker_mean, marker_scale, marker_bin):
    samples, markers = genotypes.shape
    probes = probe_signs.shape[0]
    half = probes // 2
    devices = lax.axis_size("samp")
    total = samples * devices
    side = (lax.population_count(lax.axis_index("samp")) & 1).astype(jnp.int32).reshape(1)
    markers_info = [x.reshape(1, markers) for x in (marker_mean, marker_scale, marker_bin)]
    pheno = phenotype.reshape(1, samples)
    smem = pl.BlockSpec(memory_space=pltpu.SMEM)
    vmem = pl.BlockSpec(memory_space=pltpu.VMEM)
    hbm = pl.BlockSpec(memory_space=pl.ANY)

    width = markers // 2
    chunk = min(samples, 128)
    narrow = jax.ShapeDtypeStruct((samples, width), BF16)

    part = jax.ShapeDtypeStruct((half, width + LANES), F32)
    raw = [pltpu.VMEM((samples, width), jnp.int32)]
    acc = [pltpu.VMEM((probes + 16, width), F32)]
    sems = [pltpu.SemaphoreType.DMA((samples // chunk,))]

    def local(kernel, name, out_shape, scratch, work, moved, mib, *operands, **options):
        spaces = {id(side): smem, id(genotypes): hbm}
        return pl.pallas_call(
            functools.partial(kernel, **options),
            out_shape=out_shape,
            in_specs=[spaces.get(id(x), vmem) for x in operands],
            out_specs=jax.tree.map(lambda _: vmem, out_shape),
            scratch_shapes=scratch,
            cost_estimate=pl.CostEstimate(flops=2 * work * samples * width, bytes_accessed=moved, transcendentals=0),
            compiler_params=pltpu.CompilerParams(vmem_limit_bytes=mib * MIB),
            name=name,
        )(*operands)

    flips = [1 << b for b in range(1, devices.bit_length() - 1)]
    large = 6 * samples * width
    narrow_a = local(narrow_kernel, "narrow_first", narrow, raw + sems, 0, large, 47, genotypes, start=0, chunk=chunk)
    own_a, other_a = local(
        first_sums_kernel, "sums_first", (part, part), acc, probes, 2 * samples * width, 32, side, narrow_a, probe_signs, pheno
    )
    own_b, other_b, narrow_b = local(
        second_sums_kernel,
        "sums_second",
        (part, part, narrow),
        raw + acc + sems,
        probes,
        large,
        47,
        side,
        genotypes,
        probe_signs,
        pheno,
        start=width,
        chunk=chunk,
    )
    own_a = own_a + exchange(other_a, 1)
    own_b = own_b + exchange(other_b, 1)
    turned, back = flips[1:] + flips[:1], flips[-1:] + flips[:-1]
    received = None
    for a_even, a_odd, b_even, b_odd in zip(turned, flips, back, flips):
        own_a = own_a + exchange(own_a, a_even | 1, a_odd | 1)
        if received is not None:
            own_b = own_b + received
        received = exchange(own_b, b_even | 1, b_odd | 1)

    norm = (total * (markers // BINS)) ** -0.5
    gram_norm = 1.0 / total
    rows = half * BINS
    packed = rows // LANES * 3 * LANES // 2
    probe_rows = jax.ShapeDtypeStruct((half, BINS, samples), F32)

    def multiply(kernel, name, count, out_shape, *operands, **options):
        scratch = [pltpu.VMEM((2 * count, width), BF16)]
        return local(kernel, name, out_shape, scratch, 2 * count, 4 * count * samples, 32, *operands, norm=norm, **options)

    other_a = exchange(own_a, 1)
    own_part, other_part = (
        multiply(part_kernel, name, count, jax.ShapeDtypeStruct((count, samples), F32), x, narrow_a, *markers_info, pheno=count > rows)
        for name, count, x in (("products_part", rows, own_a), ("products_part_other", rows + BINS, other_a))
    )
    own_b, received, other_part = lax.optimization_barrier((own_b, received, other_part))
    own_b = own_b + received
    other_b = exchange(own_b, 1)
    out_shape = (
        probe_rows,
        jax.ShapeDtypeStruct((1, BINS, samples), F32),
        jax.ShapeDtypeStruct((BINS // 2, packed + LANES), F32),
    )
    mine, last, gram = multiply(
        own_kernel, "products_own", rows + BINS, out_shape, own_part, other_part, own_b, narrow_b, *markers_info, gram_norm=gram_norm
    )
    out_shape = (probe_rows, jax.ShapeDtypeStruct((BINS // 2, 2 * packed + LANES), F32))
    theirs, gram = multiply(
        other_kernel, "products_other", rows, out_shape, side, other_part, other_b, narrow_b, *markers_info, gram, gram_norm=gram_norm
    )
    products = pl.pallas_call(
        store_kernel,
        out_shape=jax.ShapeDtypeStruct((probes + 1, BINS, samples), F32),
        in_specs=[smem, vmem, vmem, vmem],
        out_specs=hbm,
        scratch_shapes=[pltpu.SemaphoreType.DMA((3,))],
        cost_estimate=pl.CostEstimate(flops=0, bytes_accessed=4 * (probes + 1) * BINS * samples, transcendentals=0),
        compiler_params=pltpu.CompilerParams(vmem_limit_bytes=16 * MIB),
        name="products_store",
    )(side, mine, theirs, last)

    gram = gram + exchange(gram, 1)
    rest = flips
    while len(rest) > 1:
        near, far, both = (exchange(gram, f | 1) for f in (rest[0], rest[1], rest[0] | rest[1]))
        gram = (gram + near) + (far + both)
        rest = rest[2:]
    last = exchange(gram, rest[0] | 1) if rest else jnp.zeros_like(gram)
    count = (probes + 1) * BINS
    gram = pl.pallas_call(
        functools.partial(unpack_kernel, pairs=2 * rows // (2 * LANES)),
        out_shape=jax.ShapeDtypeStruct((BINS, BINS, probes + 1), F32),
        in_specs=[vmem, vmem],
        out_specs=vmem,
        scratch_shapes=[pltpu.VMEM((count, BINS // 2), F32), pltpu.VMEM((count, BINS // 2), F32)],
        compiler_params=pltpu.CompilerParams(vmem_limit_bytes=16 * MIB),
        name="gram_unpack",
    )(gram, last)
    return (products.transpose(1, 0, 2), gram)


def solution(mesh):
    in_specs = (
        P(("grp", "samp"), None),
        P(None, ("grp", "samp")),
        P(("grp", "samp")),
        P(),
        P(),
        P(),
    )
    out_specs = (P(None, None, ("grp", "samp")), P("grp", None, None))
    return jax.shard_map(shards, mesh=mesh, in_specs=in_specs, out_specs=out_specs, check_vma=False)
```

```python
import functools

import jax
import jax.numpy as jnp
from jax import lax
from jax.experimental import pallas as pl
from jax.experimental.pallas import tpu as pltpu
from jax.sharding import PartitionSpec as P

BINS = 16
LANES = 128
GROUP = LANES // BINS
F32 = jnp.float32
BF16 = jnp.bfloat16
MIB = 2**20

dot_nt = functools.partial(lax.dot_general, dimension_numbers=(((1,), (1,)), ((), ())), preferred_element_type=F32)


def two_parts(x):
    hi = x.astype(BF16)
    return hi, (x - hi.astype(F32)).astype(BF16)


def sign_rows(signs_ref):
    return (2 * signs_ref[...] - 1).astype(F32).astype(BF16)


def pheno_rows(pheno_ref):
    pheno = pheno_ref[...]
    high = pheno.astype(BF16).astype(F32)
    rest = pheno - high
    middle = rest.astype(BF16).astype(F32)
    tail = jnp.zeros((13, pheno.shape[1]), F32)
    return jnp.concatenate([high, middle, rest - middle, tail], axis=0).astype(BF16)


def add_three(x):
    return x[:1] + x[1:2] + x[2:3]


def narrowed(geno_hbm, narrow_ref, raw, sems, start, chunk):
    samples, markers = raw.shape
    rows = [slice(c * chunk, (c + 1) * chunk) for c in range(samples // chunk)]
    copies = [pltpu.make_async_copy(geno_hbm.at[s, start : start + markers], raw.at[s], sems.at[c]) for c, s in enumerate(rows)]
    for copy in copies:
        copy.start()

    def finish():
        for copy, s in zip(copies, rows):
            copy.wait()
            narrow = raw[s].astype(F32).astype(BF16)
            narrow_ref[s] = narrow
            yield s, narrow

    return finish


def place_rows(side, vectors, acc, own_ref, other_ref):
    half = own_ref.shape[0]
    probes = 2 * half
    markers = acc.shape[1]
    tiles = markers // LANES
    sums = dot_nt(jnp.ones((8, vectors.shape[1]), BF16), vectors)[:1]
    last = sums[:, probes : probes + 1] + sums[:, probes + 1 : probes + 2] + sums[:, probes + 2 : probes + 3]
    pheno = add_three(acc[probes : probes + 8, :])
    for ref, which in ((own_ref, side), (other_ref, 1 - side)):
        ref[:, :markers] = acc[pl.ds(pl.multiple_of(which * half, half), half), :]
        ref[: half - tiles, markers:] = jnp.zeros((half - tiles, LANES), F32)
        ref[:1, markers : markers + half] = jnp.where(which == 0, sums[:, :half], sums[:, half:probes])
        ref[:1, markers + half : markers + half + 1] = last
        for t in range(tiles):
            ref[half - tiles + t : half - tiles + t + 1, markers:] = pheno[:, t * LANES : (t + 1) * LANES]


def vector_rows(signs_ref, pheno_ref):
    return jnp.concatenate([sign_rows(signs_ref), pheno_rows(pheno_ref)], axis=0)


def narrow_kernel(geno_hbm, narrow_ref, raw, sems, *, start, chunk):
    for _ in narrowed(geno_hbm, narrow_ref, raw, sems, start, chunk)():
        pass


def first_sums_kernel(side_ref, narrow_ref, signs_ref, pheno_ref, own_ref, other_ref, acc):
    vectors = vector_rows(signs_ref, pheno_ref)
    acc[...] = jnp.dot(vectors, narrow_ref[...], preferred_element_type=F32)
    place_rows(side_ref[0], vectors, acc, own_ref, other_ref)


def second_sums_kernel(side_ref, geno_hbm, signs_ref, pheno_ref, own_ref, other_ref, narrow_ref, raw, acc, sems, *, start, chunk):
    finish = narrowed(geno_hbm, narrow_ref, raw, sems, start, chunk)
    vectors = vector_rows(signs_ref, pheno_ref)
    for s, narrow in finish():
        part = jnp.dot(vectors[:, s], narrow, preferred_element_type=F32)
        if s.start == 0:
            acc[...] = part
        else:
            acc[...] += part
    place_rows(side_ref[0], vectors, acc, own_ref, other_ref)


class Half:
    def __init__(self, mean_ref, scale_ref, bin_ref, geno_ref, start, norm):
        markers = geno_ref.shape[1]
        self.geno = geno_ref
        self.mean = mean_ref[:, start : start + markers]
        scale = scale_ref[:, start : start + markers]
        self.scale = scale * scale * norm
        self.member = (bin_ref[:, start : start + markers] == lax.broadcasted_iota(jnp.int32, (BINS, markers), 0)).astype(F32)

    def scores(self, sums, total):
        return (sums - self.mean * total) * self.scale

    def probe_scores(self, ref):
        markers = self.mean.shape[1]
        return [self.scores(ref[r : r + 1, :markers], ref[:1, markers + r : markers + r + 1]) for r in range(ref.shape[0])]

    def pheno_scores(self, ref):
        half = ref.shape[0]
        markers = self.mean.shape[1]
        tiles = markers // LANES
        row = jnp.concatenate([ref[t : t + 1, markers:] for t in range(half - tiles, half)], axis=1)
        return self.scores(row, ref[:1, markers + half : markers + half + 1])

    def weigh(self, rows, weights):
        shifts = []
        count = len(rows) * BINS
        for r, row in enumerate(rows):
            weighted = self.member * row
            shifts.append(jnp.sum(weighted * self.mean, axis=1, keepdims=True))
            hi, lo = two_parts(weighted)
            weights[r * BINS : (r + 1) * BINS, :] = hi
            weights[count + r * BINS : count + (r + 1) * BINS, :] = lo
        return jnp.concatenate(shifts, axis=0)

    def multiply(self, weights, span=slice(None)):
        both = dot_nt(weights[...], self.geno[span, :])
        count = both.shape[0] // 2
        return both[:count] + both[count:]

    def products(self, rows, weights):
        shift = self.weigh(rows, weights)
        return self.multiply(weights) - shift


def square_of(products):
    count = products.shape[0]
    hi, lo = two_parts(products)
    both = dot_nt(jnp.concatenate([hi, lo], axis=0), hi)
    return both[:count] + (both[count:] + both[count:].T)


def gram_of(products, gram_norm):
    column = lax.broadcasted_iota(jnp.int32, (BINS, LANES), 1)
    parts = []
    for g in range(products.shape[0] // LANES):
        square = square_of(products[g * LANES : (g + 1) * LANES])
        total = square[:BINS]
        for r in range(1, GROUP):
            total = jnp.where(column // BINS == r, square[r * BINS : (r + 1) * BINS], total)
        parts.append(total * gram_norm)
    h = BINS // 2
    packed = []
    for one, two in zip(parts[::2], parts[1::2]):
        moved = pltpu.roll(two[h:], LANES - h, 1)
        packed += [one[:h], two[:h], jnp.where(column[:h] % BINS >= h, one[h:], moved)]
    return jnp.concatenate(packed, axis=1)


def unpack_kernel(one_ref, two_ref, out_ref, rows, *, pairs):
    h = BINS // 2
    count = rows.shape[0] // BINS
    packed = one_ref[...] + two_ref[...]
    tile = [packed[:, t * LANES : (t + 1) * LANES] for t in range(packed.shape[1] // LANES)]
    for p in range(pairs):
        one, two, low = tile[3 * p : 3 * p + 3]
        for i, (a, b) in enumerate(((one, low), (two, pltpu.roll(low, h, 1)))):
            at = (2 * p + i) * LANES
            rows[at : at + LANES, :] = jnp.concatenate([a, b], axis=0).T
    last = jnp.concatenate([tile[3 * pairs], pltpu.roll(tile[3 * pairs], LANES - BINS, 1)], axis=0).T
    rows[2 * pairs * LANES :, :] = last[:BINS]
    for l in range(BINS):
        plane = rows[pl.ds(l, count, stride=BINS), :].T
        if l < h:
            out_ref[:h, l, :] = plane[:h]
        else:
            out_ref[:, l, :] = plane
            out_ref[l, :h, :] = plane[:h]


def part_kernel(sums_a, geno_a, mean_ref, scale_ref, bin_ref, part_ref, weights, *, norm, pheno):
    first = Half(mean_ref, scale_ref, bin_ref, geno_a, 0, norm)
    rows = first.probe_scores(sums_a) + ([first.pheno_scores(sums_a)] if pheno else [])
    part_ref[...] = first.products(rows, weights)


def own_kernel(own_part, other_part, own_b, geno_b, mean_ref, scale_ref, bin_ref, mine_ref, last_ref, gram_ref, weights, *, norm, gram_norm):
    half = own_b.shape[0]
    count = half * BINS
    samples, markers = geno_b.shape
    second = Half(mean_ref, scale_ref, bin_ref, geno_b, markers, norm)
    parts = second.products(second.probe_scores(own_b) + [second.pheno_scores(own_b)], weights)
    mine = own_part[...] + parts[:count]
    mine_ref[...] = mine.reshape(half, BINS, samples)
    last = other_part[count:] + parts[count:]
    last_ref[0] = last
    probe_gram = gram_of(mine, gram_norm)
    gram_ref[:, : probe_gram.shape[1]] = probe_gram
    square = square_of(last) * gram_norm
    h = BINS // 2
    rest = jnp.zeros((h, LANES - 2 * BINS), F32)
    gram_ref[:, probe_gram.shape[1] :] = jnp.concatenate([square[:h], square[h:], rest], axis=1)


def other_kernel(side_ref, part_ref, other_b, geno_b, mean_ref, scale_ref, bin_ref, own_gram_ref, theirs_ref, gram_ref, weights, *, norm, gram_norm):
    half = other_b.shape[0]
    side = side_ref[0]
    samples, markers = geno_b.shape
    second = Half(mean_ref, scale_ref, bin_ref, geno_b, markers, norm)
    products = part_ref[: half * BINS] + second.products(second.probe_scores(other_b), weights)
    theirs_ref[...] = products.reshape(half, BINS, samples)
    gram = gram_of(products, gram_norm)
    packed = gram.shape[1]
    gram_ref[:, pl.ds(pl.multiple_of((1 - side) * packed, packed), packed)] = gram
    gram_ref[:, pl.ds(pl.multiple_of(side * packed, packed), packed)] = own_gram_ref[:, :packed]
    gram_ref[:, 2 * packed :] = own_gram_ref[:, packed:]


def store_kernel(side_ref, mine_ref, theirs_ref, last_ref, out_ref, sems):
    half = mine_ref.shape[0]
    copies = []
    for i, (ref, which) in enumerate(((mine_ref, side_ref[0]), (theirs_ref, 1 - side_ref[0]))):
        to = out_ref.at[pl.ds(pl.multiple_of(which * half, half), half)]
        copies.append(pltpu.make_async_copy(ref, to, sems.at[i]))
    copies.append(pltpu.make_async_copy(last_ref, out_ref.at[pl.ds(2 * half, 1)], sems.at[2]))
    for copy in copies:
        copy.start()
    for copy in copies:
        copy.wait()


def parity(i):
    return bin(i).count("1") % 2


def exchange(x, even, odd=None):
    pairs = [(i, i ^ (even if odd is None or not parity(i) else odd)) for i in range(lax.axis_size("samp"))]
    return lax.ppermute(x, "samp", pairs)


def shards(genotypes, probe_signs, phenotype, marker_mean, marker_scale, marker_bin):
    samples, markers = genotypes.shape
    probes = probe_signs.shape[0]
    half = probes // 2
    devices = lax.axis_size("samp")
    total = samples * devices
    side = (lax.population_count(lax.axis_index("samp")) & 1).astype(jnp.int32).reshape(1)
    markers_info = [x.reshape(1, markers) for x in (marker_mean, marker_scale, marker_bin)]
    pheno = phenotype.reshape(1, samples)
    smem = pl.BlockSpec(memory_space=pltpu.SMEM)
    vmem = pl.BlockSpec(memory_space=pltpu.VMEM)
    hbm = pl.BlockSpec(memory_space=pl.ANY)

    width = markers // 2
    chunk = min(samples, 128)
    narrow = jax.ShapeDtypeStruct((samples, width), BF16)

    part = jax.ShapeDtypeStruct((half, width + LANES), F32)
    raw = [pltpu.VMEM((samples, width), jnp.int32)]
    acc = [pltpu.VMEM((probes + 16, width), F32)]
    sems = [pltpu.SemaphoreType.DMA((samples // chunk,))]

    def local(kernel, name, out_shape, scratch, work, moved, mib, *operands, **options):
        spaces = {id(side): smem, id(genotypes): hbm}
        return pl.pallas_call(
            functools.partial(kernel, **options),
            out_shape=out_shape,
            in_specs=[spaces.get(id(x), vmem) for x in operands],
            out_specs=jax.tree.map(lambda _: vmem, out_shape),
            scratch_shapes=scratch,
            cost_estimate=pl.CostEstimate(flops=2 * work * samples * width, bytes_accessed=moved, transcendentals=0),
            compiler_params=pltpu.CompilerParams(vmem_limit_bytes=mib * MIB),
            name=name,
        )(*operands)

    flips = [1 << b for b in range(1, devices.bit_length() - 1)]
    large = 6 * samples * width
    narrow_a = local(narrow_kernel, "narrow_first", narrow, raw + sems, 0, large, 47, genotypes, start=0, chunk=chunk)
    own_a, other_a = local(
        first_sums_kernel, "sums_first", (part, part), acc, probes, 2 * samples * width, 32, side, narrow_a, probe_signs, pheno
    )
    own_b, other_b, narrow_b = local(
        second_sums_kernel,
        "sums_second",
        (part, part, narrow),
        raw + acc + sems,
        probes,
        large,
        47,
        side,
        genotypes,
        probe_signs,
        pheno,
        start=width,
        chunk=chunk,
    )
    own_a = own_a + exchange(other_a, 1)
    own_b = own_b + exchange(other_b, 1)
    turned, back = flips[1:] + flips[:1], flips[-1:] + flips[:-1]
    received = None
    for a_even, a_odd, b_even, b_odd in zip(turned, flips, back, flips):
        own_a = own_a + exchange(own_a, a_even | 1, a_odd | 1)
        if received is not None:
            own_b = own_b + received
        received = exchange(own_b, b_even | 1, b_odd | 1)

    norm = (total * (markers // BINS)) ** -0.5
    gram_norm = 1.0 / total
    rows = half * BINS
    packed = rows // LANES * 3 * LANES // 2
    probe_rows = jax.ShapeDtypeStruct((half, BINS, samples), F32)

    def multiply(kernel, name, count, out_shape, *operands, **options):
        scratch = [pltpu.VMEM((2 * count, width), BF16)]
        return local(kernel, name, out_shape, scratch, 2 * count, 4 * count * samples, 32, *operands, norm=norm, **options)

    other_a = exchange(own_a, 1)
    own_part, other_part = (
        multiply(part_kernel, name, count, jax.ShapeDtypeStruct((count, samples), F32), x, narrow_a, *markers_info, pheno=count > rows)
        for name, count, x in (("products_part", rows, own_a), ("products_part_other", rows + BINS, other_a))
    )
    own_b, received, other_part = lax.optimization_barrier((own_b, received, other_part))
    own_b = own_b + received
    other_b = exchange(own_b, 1)
    out_shape = (
        probe_rows,
        jax.ShapeDtypeStruct((1, BINS, samples), F32),
        jax.ShapeDtypeStruct((BINS // 2, packed + LANES), F32),
    )
    mine, last, gram = multiply(
        own_kernel, "products_own", rows + BINS, out_shape, own_part, other_part, own_b, narrow_b, *markers_info, gram_norm=gram_norm
    )
    out_shape = (probe_rows, jax.ShapeDtypeStruct((BINS // 2, 2 * packed + LANES), F32))
    theirs, gram = multiply(
        other_kernel, "products_other", rows, out_shape, side, other_part, other_b, narrow_b, *markers_info, gram, gram_norm=gram_norm
    )
    products = pl.pallas_call(
        store_kernel,
        out_shape=jax.ShapeDtypeStruct((probes + 1, BINS, samples), F32),
        in_specs=[smem, vmem, vmem, vmem],
        out_specs=hbm,
        scratch_shapes=[pltpu.SemaphoreType.DMA((3,))],
        cost_estimate=pl.CostEstimate(flops=0, bytes_accessed=4 * (probes + 1) * BINS * samples, transcendentals=0),
        compiler_params=pltpu.CompilerParams(vmem_limit_bytes=16 * MIB),
        name="products_store",
    )(side, mine, theirs, last)

    gram = gram + exchange(gram, 1)
    rest = flips
    while len(rest) > 1:
        near, far, both = (exchange(gram, f | 1) for f in (rest[0], rest[1], rest[0] | rest[1]))
        gram = (gram + near) + (far + both)
        rest = rest[2:]
    last = exchange(gram, rest[0] | 1) if rest else jnp.zeros_like(gram)
    count = (probes + 1) * BINS
    gram = pl.pallas_call(
        functools.partial(unpack_kernel, pairs=2 * rows // (2 * LANES)),
        out_shape=jax.ShapeDtypeStruct((BINS, BINS, probes + 1), F32),
        in_specs=[vmem, vmem],
        out_specs=vmem,
        scratch_shapes=[pltpu.VMEM((count, BINS), F32)],
        compiler_params=pltpu.CompilerParams(vmem_limit_bytes=16 * MIB),
        name="gram_unpack",
    )(gram, last)
    return (products.transpose(1, 0, 2), gram)


def solution(mesh):
    in_specs = (
        P(("grp", "samp"), None),
        P(None, ("grp", "samp")),
        P(("grp", "samp")),
        P(),
        P(),
        P(),
    )
    out_specs = (P(None, None, ("grp", "samp")), P("grp", None, None))
    return jax.shard_map(shards, mesh=mesh, in_specs=in_specs, out_specs=out_specs, check_vma=False)
```

```python
import functools

import jax
import jax.numpy as jnp
from jax import lax
from jax.experimental import pallas as pl
from jax.experimental.pallas import tpu as pltpu
from jax.sharding import PartitionSpec as P

BINS = 16
LANES = 128
GROUP = LANES // BINS
F32 = jnp.float32
BF16 = jnp.bfloat16
MIB = 2**20

dot_nt = functools.partial(lax.dot_general, dimension_numbers=(((1,), (1,)), ((), ())), preferred_element_type=F32)


def two_parts(x):
    hi = x.astype(BF16)
    return hi, (x - hi.astype(F32)).astype(BF16)


def sign_rows(signs_ref):
    return (2 * signs_ref[...] - 1).astype(F32).astype(BF16)


def pheno_rows(pheno_ref):
    pheno = pheno_ref[...]
    high = pheno.astype(BF16).astype(F32)
    rest = pheno - high
    middle = rest.astype(BF16).astype(F32)
    tail = jnp.zeros((13, pheno.shape[1]), F32)
    return jnp.concatenate([high, middle, rest - middle, tail], axis=0).astype(BF16)


def add_three(x):
    return x[:1] + x[1:2] + x[2:3]


def narrowed(geno_hbm, narrow_ref, raw, sems, start, chunk):
    samples, markers = raw.shape
    rows = [slice(c * chunk, (c + 1) * chunk) for c in range(samples // chunk)]
    copies = [pltpu.make_async_copy(geno_hbm.at[s, start : start + markers], raw.at[s], sems.at[c]) for c, s in enumerate(rows)]
    for copy in copies:
        copy.start()

    def finish():
        for copy, s in zip(copies, rows):
            copy.wait()
            narrow = raw[s].astype(F32).astype(BF16)
            narrow_ref[s] = narrow
            yield s, narrow

    return finish


def place_rows(side, vectors, acc, own_ref, other_ref):
    half = own_ref.shape[0]
    probes = 2 * half
    markers = acc.shape[1]
    tiles = markers // LANES
    sums = dot_nt(jnp.ones((8, vectors.shape[1]), BF16), vectors)[:1]
    last = sums[:, probes : probes + 1] + sums[:, probes + 1 : probes + 2] + sums[:, probes + 2 : probes + 3]
    pheno = add_three(acc[probes : probes + 8, :])
    for ref, which in ((own_ref, side), (other_ref, 1 - side)):
        ref[:, :markers] = acc[pl.ds(pl.multiple_of(which * half, half), half), :]
        ref[: half - tiles, markers:] = jnp.zeros((half - tiles, LANES), F32)
        ref[:1, markers : markers + half] = jnp.where(which == 0, sums[:, :half], sums[:, half:probes])
        ref[:1, markers + half : markers + half + 1] = last
        for t in range(tiles):
            ref[half - tiles + t : half - tiles + t + 1, markers:] = pheno[:, t * LANES : (t + 1) * LANES]


def vector_rows(signs_ref, pheno_ref):
    return jnp.concatenate([sign_rows(signs_ref), pheno_rows(pheno_ref)], axis=0)


def narrow_kernel(geno_hbm, narrow_ref, raw, sems, *, start, chunk):
    for _ in narrowed(geno_hbm, narrow_ref, raw, sems, start, chunk)():
        pass


def first_sums_kernel(side_ref, narrow_ref, signs_ref, pheno_ref, own_ref, other_ref, acc):
    vectors = vector_rows(signs_ref, pheno_ref)
    acc[...] = jnp.dot(vectors, narrow_ref[...], preferred_element_type=F32)
    place_rows(side_ref[0], vectors, acc, own_ref, other_ref)


def second_sums_kernel(side_ref, geno_hbm, signs_ref, pheno_ref, own_ref, other_ref, narrow_ref, raw, acc, sems, *, start, chunk):
    finish = narrowed(geno_hbm, narrow_ref, raw, sems, start, chunk)
    vectors = vector_rows(signs_ref, pheno_ref)
    for s, narrow in finish():
        part = jnp.dot(vectors[:, s], narrow, preferred_element_type=F32)
        if s.start == 0:
            acc[...] = part
        else:
            acc[...] += part
    place_rows(side_ref[0], vectors, acc, own_ref, other_ref)


class Half:
    def __init__(self, mean_ref, scale_ref, bin_ref, geno_ref, start, norm):
        markers = geno_ref.shape[1]
        self.geno = geno_ref
        self.mean = mean_ref[:, start : start + markers]
        scale = scale_ref[:, start : start + markers]
        self.scale = scale * scale * norm
        self.member = (bin_ref[:, start : start + markers] == lax.broadcasted_iota(jnp.int32, (BINS, markers), 0)).astype(F32)

    def scores(self, sums, total):
        return (sums - self.mean * total) * self.scale

    def probe_scores(self, ref):
        markers = self.mean.shape[1]
        return [self.scores(ref[r : r + 1, :markers], ref[:1, markers + r : markers + r + 1]) for r in range(ref.shape[0])]

    def pheno_scores(self, ref):
        half = ref.shape[0]
        markers = self.mean.shape[1]
        tiles = markers // LANES
        row = jnp.concatenate([ref[t : t + 1, markers:] for t in range(half - tiles, half)], axis=1)
        return self.scores(row, ref[:1, markers + half : markers + half + 1])

    def weigh(self, rows, weights):
        shifts = []
        count = len(rows) * BINS
        for r, row in enumerate(rows):
            weighted = self.member * row
            shifts.append(jnp.sum(weighted * self.mean, axis=1, keepdims=True))
            hi, lo = two_parts(weighted)
            weights[r * BINS : (r + 1) * BINS, :] = hi
            weights[count + r * BINS : count + (r + 1) * BINS, :] = lo
        return jnp.concatenate(shifts, axis=0)

    def multiply(self, weights, span=slice(None)):
        both = dot_nt(weights[...], self.geno[span, :])
        count = both.shape[0] // 2
        return both[:count] + both[count:]

    def products(self, rows, weights):
        shift = self.weigh(rows, weights)
        return self.multiply(weights) - shift


def square_of(products):
    count = products.shape[0]
    hi, lo = two_parts(products)
    both = dot_nt(jnp.concatenate([hi, lo], axis=0), hi)
    return both[:count] + (both[count:] + both[count:].T)


def gram_of(products, gram_norm):
    column = lax.broadcasted_iota(jnp.int32, (BINS, LANES), 1)
    parts = []
    for g in range(products.shape[0] // LANES):
        square = square_of(products[g * LANES : (g + 1) * LANES])
        total = square[:BINS]
        for r in range(1, GROUP):
            total = jnp.where(column // BINS == r, square[r * BINS : (r + 1) * BINS], total)
        parts.append(total * gram_norm)
    h = BINS // 2
    packed = []
    for one, two in zip(parts[::2], parts[1::2]):
        moved = pltpu.roll(two[h:], LANES - h, 1)
        packed += [one[:h], two[:h], jnp.where(column[:h] % BINS >= h, one[h:], moved)]
    return jnp.concatenate(packed, axis=1)


def unpack_kernel(one_ref, two_ref, out_ref, rows, *, pairs):
    h = BINS // 2
    count = rows.shape[0] // BINS
    packed = one_ref[...] + two_ref[...]
    tile = [packed[:, t * LANES : (t + 1) * LANES] for t in range(packed.shape[1] // LANES)]
    for p in range(pairs):
        one, two, low = tile[3 * p : 3 * p + 3]
        for i, (a, b) in enumerate(((one, low), (two, pltpu.roll(low, h, 1)))):
            at = (2 * p + i) * LANES
            rows[at : at + LANES, :] = jnp.concatenate([a, b], axis=0).T
    last = jnp.concatenate([tile[3 * pairs], pltpu.roll(tile[3 * pairs], LANES - BINS, 1)], axis=0).T
    rows[2 * pairs * LANES :, :] = last[:BINS]
    for l in range(BINS):
        plane = rows[pl.ds(l, count, stride=BINS), :].T
        if l < h:
            out_ref[:h, l, :] = plane[:h]
        else:
            out_ref[:, l, :] = plane
            out_ref[l, :h, :] = plane[:h]


def part_kernel(sums_a, geno_a, mean_ref, scale_ref, bin_ref, part_ref, weights, *, norm, pheno):
    first = Half(mean_ref, scale_ref, bin_ref, geno_a, 0, norm)
    rows = first.probe_scores(sums_a) + ([first.pheno_scores(sums_a)] if pheno else [])
    part_ref[...] = first.products(rows, weights)


def own_kernel(own_part, other_part, own_b, geno_b, mean_ref, scale_ref, bin_ref, mine_ref, last_ref, gram_ref, weights, *, norm, gram_norm):
    half = own_b.shape[0]
    count = half * BINS
    samples, markers = geno_b.shape
    second = Half(mean_ref, scale_ref, bin_ref, geno_b, markers, norm)
    parts = second.products(second.probe_scores(own_b) + [second.pheno_scores(own_b)], weights)
    mine = own_part[...] + parts[:count]
    mine_ref[...] = mine.reshape(half, BINS, samples)
    last = other_part[count:] + parts[count:]
    last_ref[0] = last
    probe_gram = gram_of(mine, gram_norm)
    gram_ref[:, : probe_gram.shape[1]] = probe_gram
    square = square_of(last) * gram_norm
    h = BINS // 2
    rest = jnp.zeros((h, LANES - 2 * BINS), F32)
    gram_ref[:, probe_gram.shape[1] :] = jnp.concatenate([square[:h], square[h:], rest], axis=1)


def other_kernel(side_ref, part_ref, other_b, geno_b, mean_ref, scale_ref, bin_ref, own_gram_ref, theirs_ref, gram_ref, weights, *, norm, gram_norm):
    half = other_b.shape[0]
    side = side_ref[0]
    samples, markers = geno_b.shape
    second = Half(mean_ref, scale_ref, bin_ref, geno_b, markers, norm)
    products = part_ref[: half * BINS] + second.products(second.probe_scores(other_b), weights)
    theirs_ref[...] = products.reshape(half, BINS, samples)
    gram = gram_of(products, gram_norm)
    packed = gram.shape[1]
    gram_ref[:, pl.ds(pl.multiple_of((1 - side) * packed, packed), packed)] = gram
    gram_ref[:, pl.ds(pl.multiple_of(side * packed, packed), packed)] = own_gram_ref[:, :packed]
    gram_ref[:, 2 * packed :] = own_gram_ref[:, packed:]


def store_kernel(side_ref, mine_ref, theirs_ref, last_ref, out_ref, sems):
    half = mine_ref.shape[0]
    copies = []
    for i, (ref, which) in enumerate(((mine_ref, side_ref[0]), (theirs_ref, 1 - side_ref[0]))):
        to = out_ref.at[pl.ds(pl.multiple_of(which * half, half), half)]
        copies.append(pltpu.make_async_copy(ref, to, sems.at[i]))
    copies.append(pltpu.make_async_copy(last_ref, out_ref.at[pl.ds(2 * half, 1)], sems.at[2]))
    for copy in copies:
        copy.start()
    for copy in copies:
        copy.wait()


def parity(i):
    return bin(i).count("1") % 2


def exchange(x, even, odd=None):
    pairs = [(i, i ^ (even if odd is None or not parity(i) else odd)) for i in range(lax.axis_size("samp"))]
    return lax.ppermute(x, "samp", pairs)


def shards(genotypes, probe_signs, phenotype, marker_mean, marker_scale, marker_bin):
    samples, markers = genotypes.shape
    probes = probe_signs.shape[0]
    half = probes // 2
    devices = lax.axis_size("samp")
    total = samples * devices
    side = (lax.population_count(lax.axis_index("samp")) & 1).astype(jnp.int32).reshape(1)
    markers_info = [x.reshape(1, markers) for x in (marker_mean, marker_scale, marker_bin)]
    pheno = phenotype.reshape(1, samples)
    smem = pl.BlockSpec(memory_space=pltpu.SMEM)
    vmem = pl.BlockSpec(memory_space=pltpu.VMEM)
    hbm = pl.BlockSpec(memory_space=pl.ANY)

    width = markers // 2
    chunk = min(samples, 128)
    narrow = jax.ShapeDtypeStruct((samples, width), BF16)

    part = jax.ShapeDtypeStruct((half, width + LANES), F32)
    raw = [pltpu.VMEM((samples, width), jnp.int32)]
    acc = [pltpu.VMEM((probes + 16, width), F32)]
    sems = [pltpu.SemaphoreType.DMA((samples // chunk,))]

    def local(kernel, name, out_shape, scratch, work, moved, mib, *operands, **options):
        spaces = {id(side): smem, id(genotypes): hbm}
        return pl.pallas_call(
            functools.partial(kernel, **options),
            out_shape=out_shape,
            in_specs=[spaces.get(id(x), vmem) for x in operands],
            out_specs=jax.tree.map(lambda _: vmem, out_shape),
            scratch_shapes=scratch,
            cost_estimate=pl.CostEstimate(flops=2 * work * samples * width, bytes_accessed=moved, transcendentals=0),
            compiler_params=pltpu.CompilerParams(vmem_limit_bytes=mib * MIB),
            name=name,
        )(*operands)

    flips = [1 << b for b in range(1, devices.bit_length() - 1)]
    large = 6 * samples * width
    narrow_a = local(narrow_kernel, "narrow_first", narrow, raw + sems, 0, large, 47, genotypes, start=0, chunk=chunk)
    own_a, other_a = local(
        first_sums_kernel, "sums_first", (part, part), acc, probes, 2 * samples * width, 32, side, narrow_a, probe_signs, pheno
    )
    own_b, other_b, narrow_b = local(
        second_sums_kernel,
        "sums_second",
        (part, part, narrow),
        raw + acc + sems,
        probes,
        large,
        47,
        side,
        genotypes,
        probe_signs,
        pheno,
        start=width,
        chunk=chunk,
    )
    own_a = own_a + exchange(other_a, 1)
    own_b = own_b + exchange(other_b, 1)
    turned, back = flips[1:] + flips[:1], flips[-1:] + flips[:-1]
    received = None
    for a_even, a_odd, b_even, b_odd in zip(turned, flips, back, flips):
        own_a = own_a + exchange(own_a, a_even | 1, a_odd | 1)
        if received is not None:
            own_b = own_b + received
        received = exchange(own_b, b_even | 1, b_odd | 1)

    norm = (total * (markers // BINS)) ** -0.5
    gram_norm = 1.0 / total
    rows = half * BINS
    packed = rows // LANES * 3 * LANES // 2
    probe_rows = jax.ShapeDtypeStruct((half, BINS, samples), F32)

    def multiply(kernel, name, count, out_shape, *operands, **options):
        scratch = [pltpu.VMEM((2 * count, width), BF16)]
        return local(kernel, name, out_shape, scratch, 2 * count, 4 * count * samples, 32, *operands, norm=norm, **options)

    other_a = exchange(own_a, 1)
    own_part, other_part = (
        multiply(part_kernel, name, count, jax.ShapeDtypeStruct((count, samples), F32), x, narrow_a, *markers_info, pheno=count > rows)
        for name, count, x in (("products_part", rows, own_a), ("products_part_other", rows + BINS, other_a))
    )
    received, own_part, other_part = lax.optimization_barrier((received, own_part, other_part))
    own_b = own_b + received
    other_b = exchange(own_b, 1)
    out_shape = (
        probe_rows,
        jax.ShapeDtypeStruct((1, BINS, samples), F32),
        jax.ShapeDtypeStruct((BINS // 2, packed + LANES), F32),
    )
    mine, last, gram = multiply(
        own_kernel, "products_own", rows + BINS, out_shape, own_part, other_part, own_b, narrow_b, *markers_info, gram_norm=gram_norm
    )
    out_shape = (probe_rows, jax.ShapeDtypeStruct((BINS // 2, 2 * packed + LANES), F32))
    theirs, gram = multiply(
        other_kernel, "products_other", rows, out_shape, side, other_part, other_b, narrow_b, *markers_info, gram, gram_norm=gram_norm
    )
    products = pl.pallas_call(
        store_kernel,
        out_shape=jax.ShapeDtypeStruct((probes + 1, BINS, samples), F32),
        in_specs=[smem, vmem, vmem, vmem],
        out_specs=hbm,
        scratch_shapes=[pltpu.SemaphoreType.DMA((3,))],
        cost_estimate=pl.CostEstimate(flops=0, bytes_accessed=4 * (probes + 1) * BINS * samples, transcendentals=0),
        compiler_params=pltpu.CompilerParams(vmem_limit_bytes=16 * MIB),
        name="products_store",
    )(side, mine, theirs, last)

    gram = gram + exchange(gram, 1)
    rest = flips
    while len(rest) > 1:
        near, far, both = (exchange(gram, f | 1) for f in (rest[0], rest[1], rest[0] | rest[1]))
        gram = (gram + near) + (far + both)
        rest = rest[2:]
    last = exchange(gram, rest[0] | 1) if rest else jnp.zeros_like(gram)
    count = (probes + 1) * BINS
    gram = pl.pallas_call(
        functools.partial(unpack_kernel, pairs=2 * rows // (2 * LANES)),
        out_shape=jax.ShapeDtypeStruct((BINS, BINS, probes + 1), F32),
        in_specs=[vmem, vmem],
        out_specs=vmem,
        scratch_shapes=[pltpu.VMEM((count, BINS), F32)],
        compiler_params=pltpu.CompilerParams(vmem_limit_bytes=16 * MIB),
        name="gram_unpack",
    )(gram, last)
    return (products.transpose(1, 0, 2), gram)


def solution(mesh):
    in_specs = (
        P(("grp", "samp"), None),
        P(None, ("grp", "samp")),
        P(("grp", "samp")),
        P(),
        P(),
        P(),
    )
    out_specs = (P(None, None, ("grp", "samp")), P("grp", None, None))
    return jax.shard_map(shards, mesh=mesh, in_specs=in_specs, out_specs=out_specs, check_vma=False)
```
